32 devices in a mesh: dp: 2 (over y), ctx: 4 (over x, core), tensor: 4 (over z).
Axes of the slice: x: 2, y: 2, z: 4, core: 2. Of those that a mesh axis runs over, the one named last changes fastest.
Arguments:
- hidden_in: bfloat16 [2, 2048, 2048], P('dp', 'ctx'), may hold values from -6 to 6
- positions: int32 [2, 2048], P('dp'), may hold values from 0 to 2047, as said below
- cotangent: bfloat16 [2, 2048, 2048], P('dp', 'ctx'), may hold values from -6 to 6
- w_qkv: float32 [2048, 3072], P(('dp', 'ctx'), 'tensor'), may hold values from -0.15625 to 0.15625
- w_qkv_first: float32 [2048, 3072], P(('dp', 'ctx'), 'tensor'), may hold values from -40 to 40
- w_qkv_second: float32 [2048, 3072], P(('dp', 'ctx'), 'tensor'), may hold values from 217.088 to 860.16
- w_out: float32 [2048, 2048], P('tensor', ('dp', 'ctx')), may hold values from -0.75 to 0.75
- w_out_first: float32 [2048, 2048], P('tensor', ('dp', 'ctx')), may hold values from -4 to 4
- w_out_second: float32 [2048, 2048], P('tensor', ('dp', 'ctx')), may hold values from 0.625 to 2.5
- w_gate_up: float32 [2048, 16384], P(('dp', 'ctx'), 'tensor'), may hold values from -0.125 to 0.125
- w_gate_up_first: float32 [2048, 16384], P(('dp', 'ctx'), 'tensor'), may hold values from -12 to 12
- w_gate_up_second: float32 [2048, 16384], P(('dp', 'ctx'), 'tensor'), may hold values from 19.6608 to 77.824
- w_down: float32 [8192, 2048], P('tensor', ('dp', 'ctx')), may hold values from -0.0625 to 0.0625
- w_down_first: float32 [8192, 2048], P('tensor', ('dp', 'ctx')), may hold values from -24 to 24
- w_down_second: float32 [8192, 2048], P('tensor', ('dp', 'ctx')), may hold values from 77.824 to 311.296
- norm_gains: float32 [2, 2048], P(None, ('dp', 'ctx')), may hold values from 0.1 to 1.9
- norm_gains_first: float32 [2, 2048], P(None, ('dp', 'ctx')), may hold values from -40 to 40
- norm_gains_second: float32 [2, 2048], P(None, ('dp', 'ctx')), may hold values from 217.088 to 860.16
Outputs:
- block_out: bfloat16 [2, 2048, 2048], P('dp', 'ctx')
- grad_in: float32 [2, 2048, 2048], P('dp', 'ctx')
- w_qkv_first_new: float32 [2048, 3072], P(('dp', 'ctx'), 'tensor')
- w_qkv_second_new: float32 [2048, 3072], P(('dp', 'ctx'), 'tensor')
- w_qkv_new: float32 [2048, 3072], P(('dp', 'ctx'), 'tensor')
- w_out_first_new: float32 [2048, 2048], P('tensor', ('dp', 'ctx'))
- w_out_second_new: float32 [2048, 2048], P('tensor', ('dp', 'ctx'))
- w_out_new: float32 [2048, 2048], P('tensor', ('dp', 'ctx'))
- w_gate_up_first_new: float32 [2048, 16384], P(('dp', 'ctx'), 'tensor')
- w_gate_up_second_new: float32 [2048, 16384], P(('dp', 'ctx'), 'tensor')
- w_gate_up_new: float32 [2048, 16384], P(('dp', 'ctx'), 'tensor')
- w_down_first_new: float32 [8192, 2048], P('tensor', ('dp', 'ctx'))
- w_down_second_new: float32 [8192, 2048], P('tensor', ('dp', 'ctx'))
- w_down_new: float32 [8192, 2048], P('tensor', ('dp', 'ctx'))
- norm_gains_first_new: float32 [2, 2048], P(None, ('dp', 'ctx'))
- norm_gains_second_new: float32 [2, 2048], P(None, ('dp', 'ctx'))
- norm_gains_new: float32 [2, 2048], P(None, ('dp', 'ctx'))
The draws below stay inside these ranges and needn't reach their ends.
Inputs may be any that keep to these rules, and one draw needn't show every extreme that they name: Each row is a permutation of the positions of one sequence, made of aligned runs of 256 tokens holding consecutive rising positions, each run starting at a multiple of 256.
All inputs are finite; a program needn't handle non-finite values.
Results may differ from the reference program's by a relative error of at most 0.015.
The reference program's roundings to bfloat16 on the way count: a program that leaves them out, or rounds other values in their place, can miss the bound.
Values may be sent and summed in bfloat16 or wider, within the bound.
No kernel may reach another device: no remote copies, remote signals or barrier semaphores. Data moves between devices by JAX's collectives and lax.ppermute only.
A program may use at most 256 MiB of HBM per device.

```python
import math
import jax
import jax.numpy as jnp
from jax import lax

D = 2048
HQ = 32
KV = 8
HD = 64
FF = 8192
TOK_DEV = 512
STEP = 10
SEQ_LEN = 2048
SEQS = 2
TOKENS = 4096
N_CTX = 4
N_TENSOR = 4


def shuffle_runs(one_key):
    return jax.random.permutation(one_key, 2 * N_CTX)


def draw_positions(key, part):
    key = jax.random.fold_in(key, 7)
    half_run = TOK_DEV // 2
    seq_keys = jax.random.split(key, SEQS)
    run_order = jax.vmap(shuffle_runs)(seq_keys).astype(jnp.int32)
    offsets = jnp.arange(half_run, dtype=jnp.int32)
    return (run_order[:, :, None] * half_run + offsets[None, None, :]).reshape(SEQS, SEQ_LEN)


def shard_levels(stream_key, extent, cuts, low, high):
    def one(dim, blocks):
        heights = jax.random.uniform(jax.random.fold_in(jax.random.fold_in(stream_key, 6), dim), (blocks,), jnp.float32, low / len(cuts), high / len(cuts))
        return jnp.repeat(jnp.exp(heights), extent[dim] // blocks).reshape((-1,) + (1,) * (len(extent) - dim - 1))

    gain = one(*cuts[0])
    for cut in cuts[1:]:
        gain = gain * one(*cut)
    return gain


def gaussian(key, dims, deviation, most, shards=(), held_as=jnp.bfloat16):
    values = jax.random.normal(key, dims, jnp.float32) * deviation
    if len(shards) > 0:
        values = shard_levels(key, dims, shards, -0.22, 0.18) * values
    return jnp.clip(values, min=-most, max=most).astype(held_as)


def setup_inputs(seed: int = 0) -> dict:
    keys = jax.random.split(jax.random.key(seed), 19)
    return {
        "hidden_in": gaussian(keys[0], (SEQS, SEQ_LEN, D), 1.0, 6.0, ((0, 2), (1, 4))),
        "positions": draw_positions(jax.random.fold_in(keys[18], 71), 0),
        "cotangent": gaussian(keys[2], (SEQS, SEQ_LEN, D), 1.0, 6.0, ((0, 2), (1, 4))),
        "w_qkv": gaussian(keys[3], (D, (HQ + 2 * KV) * HD), (D * HD ** 0.5 // 12) ** -0.5, 0.15625, ((0, 8), (1, 4)), jnp.float32),
        "w_qkv_first": gaussian(keys[4], (D, (HQ + 2 * KV) * HD), (0.11 * TOKENS ** 0.5), 40.0, ((0, 8), (1, 4)), jnp.float32),
        "w_qkv_second": jnp.clip(jnp.exp(math.log(860.16) - 1.3768156 * jax.random.uniform(keys[5], (D, (HQ + 2 * KV) * HD), jnp.float32) ** shard_levels(keys[5], (D, (HQ + 2 * KV) * HD), ((0, 8), (1, 4)), -0.2, 0.2)), 217.088, 860.16),
        "w_out": gaussian(keys[6], (HQ * HD, D), (max(1, min(HQ * HD // 8, HQ * HD * 64 // (TOK_DEV * N_CTX)))) ** -0.5, 0.75, ((0, 4), (1, 8)), jnp.float32),
        "w_out_first": gaussian(keys[7], (HQ * HD, D), (0.77 * (SEQS / HD ** 0.5) ** 0.5), 4.0, ((0, 4), (1, 8)), jnp.float32),
        "w_out_second": jnp.clip(jnp.exp(math.log(2.5) - 1.3862944 * jax.random.uniform(keys[8], (HQ * HD, D), jnp.float32) ** shard_levels(keys[8], (HQ * HD, D), ((0, 4), (1, 8)), -0.2, 0.2)), 0.625, 2.5),
        "w_gate_up": gaussian(keys[9], (D, 2 * FF), D ** -0.5, 0.125, ((0, 8), (1, 4)), jnp.float32),
        "w_gate_up_first": gaussian(keys[10], (D, 2 * FF), (0.033 * TOKENS ** 0.5), 12.0, ((0, 8), (1, 4)), jnp.float32),
        "w_gate_up_second": jnp.clip(jnp.exp(math.log(77.824) - 1.375823 * jax.random.uniform(keys[11], (D, 2 * FF), jnp.float32) ** shard_levels(keys[11], (D, 2 * FF), ((0, 8), (1, 4)), -0.2, 0.2)), 19.6608, 77.824),
        "w_down": gaussian(keys[12], (FF, D), FF ** -0.5, 0.0625, ((0, 4), (1, 8)), jnp.float32),
        "w_down_first": gaussian(keys[13], (FF, D), (0.066 * TOKENS ** 0.5), 24.0, ((0, 4), (1, 8)), jnp.float32),
        "w_down_second": jnp.clip(jnp.exp(math.log(311.296) - 1.3862944 * jax.random.uniform(keys[14], (FF, D), jnp.float32) ** shard_levels(keys[14], (FF, D), ((0, 4), (1, 8)), -0.2, 0.2)), 77.824, 311.296),
        "norm_gains": jnp.clip(1.0 + 0.18 * jax.random.normal(keys[15], (2, D), jnp.float32), 0.1, 1.9),
        "norm_gains_first": gaussian(keys[16], (2, D), (0.11 * TOKENS ** 0.5), 40.0, ((1, 8),), jnp.float32),
        "norm_gains_second": jnp.clip(jnp.exp(math.log(860.16) - 1.3768156 * jax.random.uniform(keys[17], (2, D), jnp.float32) ** shard_levels(keys[17], (2, D), ((1, 8),), -0.2, 0.2)), 217.088, 860.16),
    }


NORM_EPS = 1e-05
ROPE_THETA = 500000.0
SCORE_SCALE = 0.125
LEARN_RATE = 0.01
OUT_RATE = 0.05
GAIN_RATE = 0.25
BETA_ONE = 0.9
BETA_TWO = 0.95
ADAM_EPS = 1e-08
WEIGHT_DECAY = 0.1

@jax.custom_vjp
def low(v):
    return lax.optimization_barrier(v.astype(jnp.bfloat16)).astype(jnp.float32)

@jax.custom_vjp
def low_back(v):
    return v

def low_keep(v):
    return (low(v), None)

def low_pass(kept, grad):
    return (grad,)

def back_keep(v):
    return (v, None)

def back_low(kept, grad):
    return (low(grad),)
low.defvjp(low_keep, low_pass)
low_back.defvjp(back_keep, back_low)

def exact_dot(left, right):
    return jnp.dot(left, right, precision=lax.Precision.HIGHEST, preferred_element_type=jnp.float32)

def rotate(vectors, places, flip_sign):
    half = vectors.shape[-1] // 2
    freqs = ROPE_THETA ** (-(jnp.arange(half, dtype=jnp.float32) * 2.0 / vectors.shape[-1]))
    angles = places.astype(jnp.float32)[:, None] * freqs[None, :]
    cosine = jnp.cos(angles)[:, None, :]
    sine = flip_sign * jnp.sin(angles)[:, None, :]
    first = vectors[..., :half]
    second = vectors[..., half:]
    return jnp.concatenate([first * cosine - second * sine, second * cosine + first * sine], axis=-1)

def normalize(values, gain_row):
    return values * lax.rsqrt(lax.optimization_barrier(jnp.mean(values * values, axis=-1, keepdims=True)) + NORM_EPS) * gain_row

def sequence(x_seq, places, w_qkv, w_out, w_gate_up, w_down, norm_gains):
    length = x_seq.shape[0]
    heads_group = HQ // N_TENSOR
    kv_group = KV // N_TENSOR
    head_ratio = HQ // KV
    units_group = FF // N_TENSOR
    normed_one = low(normalize(x_seq, norm_gains[0]))
    projected = low_back(exact_dot(normed_one, w_qkv)).reshape(length, N_TENSOR, heads_group + 2 * kv_group, HD)
    queries = low(rotate(projected[:, :, :heads_group].reshape(length, HQ, HD), places, 1.0))
    key_rows = low(rotate(projected[:, :, heads_group:heads_group + kv_group].reshape(length, KV, HD), places, 1.0))
    value_rows = low(projected[:, :, heads_group + kv_group:].reshape(length, KV, HD))
    block_len = min(512, length)
    block_count = length // block_len

    def attend(blocks_in):
        query_block, place_block = blocks_in
        scores = low_back(jnp.einsum('qgrd,kgd->grqk', query_block, key_rows, precision=lax.Precision.HIGHEST) * SCORE_SCALE)
        visible = places[None, :] <= place_block[:, None]
        scores = jnp.where(visible[None, None], scores, -1e+30)
        highest = lax.optimization_barrier(jnp.max(scores, axis=-1, keepdims=True))
        expo = jnp.exp(scores - highest)
        probabilities = low(expo / lax.optimization_barrier(jnp.sum(expo, axis=-1, keepdims=True)))
        return jnp.einsum('grqk,kgd->qgrd', probabilities, value_rows, precision=lax.Precision.HIGHEST)
    mixed_heads = lax.map(jax.checkpoint(attend), (queries.reshape(block_count, block_len, KV, head_ratio, HD), places.reshape(block_count, block_len)))
    attn_in = low(low_back(mixed_heads.reshape(length, HQ * HD)))
    middle = x_seq + low_back(exact_dot(attn_in, w_out))
    normed_two = low(normalize(middle, norm_gains[1]))
    gate_up = low_back(exact_dot(normed_two, w_gate_up)).reshape(length, N_TENSOR, 2, units_group)
    activated = low((jax.nn.silu(gate_up[:, :, 0]) * gate_up[:, :, 1]).reshape(length, FF))
    return middle + low_back(exact_dot(activated, w_down))

def layer_forward(hidden, w_qkv, w_out, w_gate_up, w_down, norm_gains, positions):
    low_qkv = low(w_qkv)
    low_out = low(w_out)
    low_gate_up = low(w_gate_up)
    low_down = low(w_down)
    low_gains = low(norm_gains)

    def one_sequence(pair_in):
        return sequence(pair_in[0], pair_in[1], low_qkv, low_out, low_gate_up, low_down, low_gains)
    return lax.map(jax.checkpoint(one_sequence), (hidden, positions))

def adamw_step(weight, first, second, gradient, step_rate, decay_rate):
    first_new = BETA_ONE * first + (1.0 - BETA_ONE) * gradient
    second_new = BETA_TWO * second + (1.0 - BETA_TWO) * gradient * gradient
    first_hat = first_new / (1.0 - BETA_ONE ** STEP)
    second_hat = second_new / (1.0 - BETA_TWO ** STEP)
    weight_new = weight - step_rate * (first_hat / (jnp.sqrt(second_hat) + ADAM_EPS) + decay_rate * weight)
    return (first_new, second_new, weight_new)

def reference(hidden_in, positions, cotangent, w_qkv, w_qkv_first, w_qkv_second, w_out, w_out_first, w_out_second, w_gate_up, w_gate_up_first, w_gate_up_second, w_down, w_down_first, w_down_second, norm_gains, norm_gains_first, norm_gains_second):

    def forward(hidden, qkv_in, out_in, gate_up_in, down_in, gains_in):
        return layer_forward(hidden, qkv_in, out_in, gate_up_in, down_in, gains_in, positions)
    result, pullback = jax.vjp(forward, hidden_in.astype(jnp.float32), w_qkv, w_out, w_gate_up, w_down, norm_gains)
    grad_in, grad_qkv, grad_out, grad_gate_up, grad_down, grad_gains = pullback(cotangent.astype(jnp.float32))
    qkv_first, qkv_second, qkv_new = adamw_step(w_qkv, w_qkv_first, w_qkv_second, grad_qkv, LEARN_RATE, WEIGHT_DECAY)
    out_first, out_second, out_new = adamw_step(w_out, w_out_first, w_out_second, grad_out, OUT_RATE, WEIGHT_DECAY)
    gu_first, gu_second, gu_new = adamw_step(w_gate_up, w_gate_up_first, w_gate_up_second, grad_gate_up, LEARN_RATE, WEIGHT_DECAY)
    down_first, down_second, down_new = adamw_step(w_down, w_down_first, w_down_second, grad_down, LEARN_RATE, WEIGHT_DECAY)
    gain_first, gain_second, gain_new = adamw_step(norm_gains, norm_gains_first, norm_gains_second, grad_gains, GAIN_RATE, 0.0)
    return (result.astype(jnp.bfloat16), grad_in, qkv_first, qkv_second, qkv_new, out_first, out_second, out_new, gu_first, gu_second, gu_new, down_first, down_second, down_new, gain_first, gain_second, gain_new)
```

```python
import functools
import math

import jax
import jax.numpy as jnp
from jax import lax
from jax.experimental import pallas as pl
from jax.experimental.pallas import tpu as pltpu
from jax.sharding import PartitionSpec as P

HQ = 32
KV = 8
HD = 64
FF = 8192
STEP = 10
RUN = 256


NORM_EPS = 1e-05
ROPE_THETA = 500000.0
SCORE_SCALE = 0.125
LEARN_RATE = 0.01
OUT_RATE = 0.05
GAIN_RATE = 0.25
BETA_ONE = 0.9
BETA_TWO = 0.95
ADAM_EPS = 1e-08
WEIGHT_DECAY = 0.1

F32 = jnp.float32
LOW = jnp.bfloat16


def contract(left, right, left_dim, right_dim):
    return lax.dot_general(
        left, right, (((left_dim,), (right_dim,)), ((), ())), preferred_element_type=F32
    )


def rotary_tables(places):
    half = HD // 2
    freqs = ROPE_THETA ** (-(jnp.arange(half, dtype=F32) * 2.0 / HD))
    angles = freqs[:, None] * places.astype(F32)[None, :]
    return jnp.cos(angles), jnp.sin(angles)


def rotate(vectors, cosine, sine):
    half = HD // 2
    first = vectors[..., :half, :]
    second = vectors[..., half:, :]
    return jnp.concatenate(
        [first * cosine - second * sine, second * cosine + first * sine], axis=-2
    )


def normalize(values):
    factor = lax.rsqrt(jnp.mean(values * values, axis=-1, keepdims=True) + NORM_EPS)
    return (values * factor, factor)


def norm_back(grad_hat, x_hat, factor):
    return factor * (grad_hat - x_hat * jnp.mean(grad_hat * x_hat, axis=-1, keepdims=True))


def adamw_step(weight, first, second, gradient, step_rate, decay_rate):
    first_new = BETA_ONE * first + (1.0 - BETA_ONE) * gradient
    second_new = BETA_TWO * second + (1.0 - BETA_TWO) * gradient * gradient
    first_hat = first_new / (1.0 - BETA_ONE**STEP)
    second_hat = second_new / (1.0 - BETA_TWO**STEP)
    weight_new = weight - step_rate * (
        first_hat / (jnp.sqrt(second_hat) + ADAM_EPS) + decay_rate * weight
    )
    return (first_new, second_new, weight_new)


def shift_pairs(count, step):
    return [(i, (i + step) % count) for i in range(count)]


def flip_pairs(count, mask):
    return [(i, i ^ mask) for i in range(count)]


def cut(parts, index, rows):
    return lax.dynamic_slice_in_dim(parts, index * rows, rows)


def scatter_begin(parts, axis):
    count = lax.axis_size(axis)
    blocks = parts
    if not isinstance(parts, (list, tuple)):
        rows = parts.shape[0] // count
        blocks = [parts[step * rows : (step + 1) * rows] for step in range(count)]
    own = blocks[0]
    if count == 4:
        through = lax.ppermute(blocks[3].astype(LOW), axis, flip_pairs(count, 1))
        return [own, blocks[1].astype(LOW), through, blocks[2]]
    return [own] + [
        lax.ppermute(blocks[step].astype(LOW), axis, shift_pairs(count, step))
        for step in range(1, count)
    ]


def scatter_middle(pieces, axis):
    count = lax.axis_size(axis)
    if count == 4:
        own, near, through, far = pieces
        near, through = lax.optimization_barrier((near, through))
        joined = (far.astype(F32) + through.astype(F32)).astype(LOW)
        return [
            own,
            lax.ppermute(near, axis, flip_pairs(count, 1)),
            lax.ppermute(joined, axis, flip_pairs(count, 2)),
        ]
    return pieces


def scatter_end(pieces):
    total = pieces[0].astype(F32)
    for piece in pieces[1:]:
        total = total + piece.astype(F32)
    return total


def sum_scatter(parts, axis):
    return scatter_end(scatter_middle(scatter_begin(parts, axis), axis))


def gains_scatter(parts, axis):
    count = lax.axis_size(axis)
    here = lax.axis_index(axis)
    rows = parts.shape[0] // count
    total = cut(parts, here, rows)
    for step in range(1, count):
        piece = cut(parts, lax.rem(here + step, count), rows)
        total = total + lax.ppermute(piece, axis, shift_pairs(count, step))
    return total


def sum_everywhere(values, axis):
    count = lax.axis_size(axis)
    total = values
    for step in range(1, count):
        total = total + lax.ppermute(values, axis, shift_pairs(count, step))
    return total


def blocks_from_here(count, here, rows, values, axis=0):
    cuts = []
    for step in range(count):
        index = here ^ step if count == 4 else lax.rem(here + step, count)
        cuts.append(lax.dynamic_slice_in_dim(values, index * rows, rows, axis))
    return jnp.concatenate(cuts, axis=axis)


def axis_peers(axis):
    count, here = lax.axis_size(axis), lax.axis_index(axis)
    return jnp.stack(
        [here ^ step if count == 4 else lax.rem(here + step, count) for step in range(count)]
    ).astype(jnp.int32)


def gather_blocks(rows, axis):
    count = lax.axis_size(axis)
    if count == 4:
        near = lax.ppermute(rows, axis, flip_pairs(count, 1))
        far = lax.ppermute(rows, axis, flip_pairs(count, 2))
        near, far = lax.optimization_barrier((near, far))
        last = lax.ppermute(far, axis, flip_pairs(count, 1))
        return [rows, near, far, last]
    return [rows] + [
        lax.ppermute(rows, axis, shift_pairs(count, count - step)) for step in range(1, count)
    ]


def place_blocks(blocks, axis):
    count = lax.axis_size(axis)
    here = lax.axis_index(axis)
    size = blocks[0].shape[0]
    whole_rows = jnp.zeros((count * size,) + blocks[0].shape[1:], blocks[0].dtype)
    for step, block in enumerate(blocks):
        index = here ^ step if count == 4 else lax.rem(here + step, count)
        whole_rows = lax.dynamic_update_slice_in_dim(whole_rows, block, index * size, 0)
    return whole_rows


def spread(rows, axis):
    return place_blocks(gather_blocks(rows, axis), axis)


def block_place(order_ref, rank, per_device):
    run = order_ref[rank]
    return run // per_device, pl.multiple_of((run % per_device) * RUN, RUN)


def dot_nn(left, right):
    return jnp.dot(left, right, preferred_element_type=F32)


def dot_nt(left, right):
    return lax.dot_general(left, right, (((1,), (1,)), ((), ())), preferred_element_type=F32)


def causal_mask(columns):
    keys = lax.broadcasted_iota(jnp.int32, (RUN, columns), 0)
    queries = lax.broadcasted_iota(jnp.int32, (RUN, columns), 1) & (RUN - 1)
    return keys <= queries


def take_blocks(peer_ref, piece_refs, kvn_ref, kvt_ref):
    for block, piece_ref in enumerate(piece_refs):
        kvt_ref[peer_ref[block]] = piece_ref[0]
        kvn_ref[peer_ref[block]] = piece_ref[0].T


def head_columns(head):
    return slice(head * RUN, (head + 1) * RUN)


def forward_kernel(devices, per_device, ratio, order_ref, rank_ref, peer_ref, *refs):
    piece_refs = refs[:devices]
    q_ref, mix_ref, low_ref, lse_ref, q_pad, high, total, summed, kvn_ref, kvt_ref = refs[devices:]
    rank = rank_ref[pl.program_id(1)]

    @pl.when(pl.program_id(1) == 0)
    def _():
        take_blocks(peer_ref, piece_refs, kvn_ref, kvt_ref)

    for head in range(ratio):
        q_pad[:HD, head_columns(head)] = q_ref[0, head]
    q_pad[HD:] = jnp.zeros((HD, ratio * RUN), LOW)

    def visit(step, first):
        device, offset = block_place(order_ref, step, per_device)
        keys = kvn_ref[device, pl.ds(offset, RUN), :]
        values = kvt_ref[device, HD:, pl.ds(offset, RUN)]
        scores = dot_nn(keys, q_pad[...])
        if first:
            scores = jnp.where(causal_mask(ratio * RUN), scores, -1e30)
        top = jnp.max(scores, axis=0, keepdims=True)
        if not first:
            old = high[...]
            top = jnp.maximum(old, top)
            scale = jnp.exp(old - top)
        probs = jnp.exp(scores - top)
        row_sum = jnp.sum(probs, axis=0, keepdims=True)
        product = dot_nn(values, probs.astype(LOW))
        high[...] = top
        if first:
            total[...] = row_sum
            summed[...] = product
        else:
            total[...] = total[...] * scale + row_sum
            summed[...] = summed[...] * scale + product

    visit(rank, True)

    @pl.loop(0, rank)
    def _(step):
        visit(step, False)

    mixed = summed[...] / total[...]
    log_total = high[...] + jnp.log(total[...])
    for head in range(ratio):
        mix_ref[0, head] = mixed[:, head_columns(head)]
        low_ref[0, head] = mixed[:, head_columns(head)].astype(LOW)
        lse_ref[0, head] = log_total[:, head_columns(head)]


def backward_kernel(devices, per_device, ratio, earlier, order_ref, rank_ref, peer_ref, *refs):
    piece_refs, refs = refs[:devices], refs[devices:]
    earlier_refs, refs = refs[:earlier], refs[earlier:]
    q_ref, d_ref, mix_ref, lse_ref, cos_ref, sin_ref, dq_ref = refs[:7]
    dkv_refs = refs[7:-7]
    pads, row_dot, log_total, dq_sum, dkv_sum, kvn_ref, kvt_ref = refs[-7:]
    place = pl.program_id(0)
    rank = rank_ref[place]
    columns = ratio * RUN

    @pl.when(place == 0)
    def _():
        dkv_sum[...] = jnp.zeros_like(dkv_sum)
        take_blocks(peer_ref, piece_refs, kvn_ref, kvt_ref)

    pads[HD:, :columns] = jnp.zeros((HD, columns), LOW)
    pads[:HD, columns:] = jnp.zeros((HD, columns), LOW)
    for head in range(ratio):
        here = head_columns(head)
        pads[:HD, here] = q_ref[0, head]
        pads[HD:, head_columns(ratio + head)] = d_ref[0, head]
        row_dot[:, here] = jnp.sum(
            d_ref[0, head].astype(F32) * mix_ref[0, head], axis=0, keepdims=True
        )
        log_total[:, here] = lse_ref[0, head]

    def visit(step, first):
        device, offset = block_place(order_ref, step, per_device)
        rows = kvn_ref[device, pl.ds(offset, RUN), :]
        keys = kvt_ref[device, :HD, pl.ds(offset, RUN)]
        probs = jnp.exp(dot_nn(rows, pads[:, :columns]) - log_total[...])
        if first:
            probs = jnp.where(causal_mask(columns), probs, 0.0)
        d_probs = dot_nn(rows, pads[:, columns:])
        d_scores = (probs * (d_probs - row_dot[...])).astype(LOW)
        product = dot_nn(keys, d_scores)
        if first:
            dq_sum[...] = product
        else:
            dq_sum[...] += product
        dkv_sum[device, pl.ds(offset, RUN), :] += dot_nt(
            jnp.concatenate([d_scores, probs.astype(LOW)], axis=1), pads[...]
        )

    visit(rank, True)

    @pl.loop(0, rank)
    def _(step):
        visit(step, False)

    half = HD // 2
    for head in range(ratio):
        first = dq_sum[:half, head_columns(head)] * SCORE_SCALE
        second = dq_sum[half:, head_columns(head)] * SCORE_SCALE
        dq_ref[0, head, :half] = (first * cos_ref[...] + second * sin_ref[...]).astype(LOW)
        dq_ref[0, head, half:] = (second * cos_ref[...] - first * sin_ref[...]).astype(LOW)

    @pl.when(place == pl.num_programs(0) - 1)
    def _():
        for block, dkv_ref in enumerate(dkv_refs):
            start = 0
            if earlier:
                start = earlier_refs[block].shape[0]
                dkv_ref[:start] = earlier_refs[block][...]
            dkv_ref[start:] = dkv_sum[peer_ref[block]].T.astype(LOW)


VMEM_LIMIT = 48 * 1024 * 1024
SMALL_COST = pl.CostEstimate(flops=1000, bytes_accessed=1000, transcendentals=0)


def attend_forward(order, ranks, peers, queries, kv_blocks):
    groups, ratio, head_size, tokens = queries.shape
    devices = len(kv_blocks)
    width, per_tokens = kv_blocks[0].shape[1:]
    q_spec = pl.BlockSpec((1, ratio, HD, RUN), lambda g, i, *s: (g, 0, 0, i))
    blocks = groups * (tokens // RUN) * devices * (per_tokens // RUN) * ratio
    return pl.pallas_call(
        functools.partial(forward_kernel, devices, per_tokens // RUN, ratio),
        grid_spec=pltpu.PrefetchScalarGridSpec(
            num_scalar_prefetch=3,
            grid=(groups, tokens // RUN),
            in_specs=[pl.BlockSpec((1, width, per_tokens), lambda g, i, *s: (g, 0, 0))] * devices
            + [q_spec],
            out_specs=[
                q_spec,
                q_spec,
                pl.BlockSpec((1, ratio, 1, RUN), lambda g, i, *s: (g, 0, 0, i)),
            ],
            scratch_shapes=[
                pltpu.VMEM((2 * HD, ratio * RUN), LOW),
                pltpu.VMEM((1, ratio * RUN), F32),
                pltpu.VMEM((1, ratio * RUN), F32),
                pltpu.VMEM((HD, ratio * RUN), F32),
                pltpu.VMEM((devices, per_tokens, width), LOW),
                pltpu.VMEM((devices, width, per_tokens), LOW),
            ],
        ),
        out_shape=[
            jax.ShapeDtypeStruct(queries.shape, F32),
            jax.ShapeDtypeStruct(queries.shape, LOW),
            jax.ShapeDtypeStruct((groups, ratio, 1, tokens), F32),
        ],
        compiler_params=pltpu.CompilerParams(
            dimension_semantics=("arbitrary", "arbitrary"), vmem_limit_bytes=VMEM_LIMIT
        ),
        cost_estimate=pl.CostEstimate(
            flops=blocks * 64 * RUN * RUN * HD,
            bytes_accessed=8 * 1024 * 1024,
            transcendentals=blocks * RUN * RUN,
        ),
        name="attend_forward",
    )(order, ranks, peers, *kv_blocks, queries)


def attend_backward(
    group, order, ranks, peers, kv_blocks, earlier, queries, d_mixed, mixed, log_total, cosine,
    sine, *deps,
):
    groups, ratio, head_size, tokens = queries.shape
    devices = len(kv_blocks)
    width, per_tokens = kv_blocks[0].shape[1:]
    q_spec = pl.BlockSpec((1, ratio, HD, RUN), lambda i, *s: (group, 0, 0, i))
    table = pl.BlockSpec((HD // 2, RUN), lambda i, *s: (0, i))
    blocks = (tokens // RUN) * devices * (per_tokens // RUN) * ratio
    grown = width + (earlier[0].shape[0] if earlier else 0)
    inputs = [*kv_blocks, *earlier, queries, d_mixed, mixed, log_total, cosine, sine]
    return pl.pallas_call(
        with_deps(
            functools.partial(backward_kernel, devices, per_tokens // RUN, ratio, len(earlier)),
            len(inputs),
            len(deps),
            3,
        ),
        grid_spec=pltpu.PrefetchScalarGridSpec(
            num_scalar_prefetch=3,
            grid=(tokens // RUN,),
            in_specs=[pl.BlockSpec((1, width, per_tokens), lambda i, *s: (group, 0, 0))] * devices
            + [pl.BlockSpec(each.shape, lambda i, *s: (0, 0)) for each in earlier]
            + [q_spec] * 3
            + [pl.BlockSpec((1, ratio, 1, RUN), lambda i, *s: (group, 0, 0, i)), table, table]
            + [pl.BlockSpec(memory_space=pl.ANY)] * len(deps),
            out_specs=[pl.BlockSpec((1, ratio, HD, RUN), lambda i, *s: (0, 0, 0, i))]
            + [pl.BlockSpec((grown, per_tokens), lambda i, *s: (0, 0))] * devices,
            scratch_shapes=[
                pltpu.VMEM((2 * HD, 2 * ratio * RUN), LOW),
                pltpu.VMEM((1, ratio * RUN), F32),
                pltpu.VMEM((1, ratio * RUN), F32),
                pltpu.VMEM((HD, ratio * RUN), F32),
                pltpu.VMEM((devices, per_tokens, width), F32),
                pltpu.VMEM((devices, per_tokens, width), LOW),
                pltpu.VMEM((devices, width, per_tokens), LOW),
            ],
        ),
        out_shape=[jax.ShapeDtypeStruct((1,) + queries.shape[1:], LOW)]
        + [jax.ShapeDtypeStruct((grown, per_tokens), LOW)] * devices,
        compiler_params=pltpu.CompilerParams(
            dimension_semantics=("arbitrary",), vmem_limit_bytes=VMEM_LIMIT
        ),
        cost_estimate=pl.CostEstimate(
            flops=blocks * 128 * RUN * RUN * HD,
            bytes_accessed=8 * 1024 * 1024,
            transcendentals=blocks * RUN * RUN,
        ),
        name="attend_backward",
    )(order, ranks, peers, *inputs, *deps)


TILE = 256


def whole(shape):
    return pl.BlockSpec(shape, lambda j: (0,) * len(shape), pipeline_mode=pl.Buffered(1))


def with_deps(kernel, inputs, deps, scalars=0):
    first = scalars + inputs

    def run(*refs):
        kernel(*refs[:first], *refs[first + deps :])

    return run


def tile_call(kernel, name, tiles, in_specs, out_specs, out_shape, flops, scratch=(), deps=0):
    size = sum(math.prod(each.shape) * each.dtype.itemsize for each in out_shape)
    return pl.pallas_call(
        with_deps(kernel, len(in_specs), deps),
        grid=(tiles,),
        in_specs=list(in_specs) + [pl.BlockSpec(memory_space=pl.ANY)] * deps,
        out_specs=out_specs,
        out_shape=out_shape,
        scratch_shapes=scratch,
        compiler_params=pltpu.CompilerParams(
            dimension_semantics=("arbitrary",), vmem_limit_bytes=VMEM_LIMIT
        ),
        cost_estimate=pl.CostEstimate(
            flops=flops * 3 // 2, bytes_accessed=2 * size, transcendentals=0
        ),
        name=name,
    )


def held_until_kernel(values_ref, *refs):
    mark_ref = refs[-1]
    mark_ref[...] = jnp.zeros_like(mark_ref)


def held_until(values, *deps):
    hidden = pl.BlockSpec(memory_space=pl.ANY)
    return pl.pallas_call(
        held_until_kernel,
        in_specs=[hidden] * (1 + len(deps)),
        out_specs=[hidden, pl.BlockSpec(memory_space=pltpu.VMEM)],
        out_shape=[
            jax.ShapeDtypeStruct(values.shape, values.dtype),
            jax.ShapeDtypeStruct((8, 128), F32),
        ],
        input_output_aliases={0: 0},
        name="held_until",
    )(values, *deps)[0]


def store_blocks(out_refs, values):
    rows = out_refs[0].shape[0]
    for block, out_ref in enumerate(out_refs):
        out_ref[...] = values[block * rows : (block + 1) * rows].astype(out_ref.dtype)


def block_shapes(blocks, rows, width):
    kept = (0, 2) if blocks == 4 else (0,)
    return [
        jax.ShapeDtypeStruct((rows, width), F32 if block in kept else LOW)
        for block in range(blocks)
    ]


def ffn_both_kernel(blocks, tiles, *refs):
    x_refs = refs[:blocks]
    g_ref, gate_ref, up_ref, down_ref, gate_rows_ref, up_rows_ref = refs[blocks : blocks + 6]
    active_ref, d_gate_ref, d_up_ref = refs[blocks + 6 : blocks + 9]
    out_refs = refs[blocks + 9 : -3]
    x_all, d_gate_all, d_up_all = refs[-3:]
    step = pl.program_id(0)
    rows = x_refs[0].shape[0]

    @pl.when(step == 0)
    def _():
        for block in range(blocks):
            x_all[block * rows : (block + 1) * rows] = x_refs[block][...]

    @pl.when(step < tiles)
    def _():
        gate = dot_nn(x_all[...], gate_ref[...])
        up = dot_nn(x_all[...], up_ref[...])
        d_act = dot_nn(g_ref[...], down_ref[...])
        sigmoid = 1.0 / (1.0 + jnp.exp(-gate))
        silu = gate * sigmoid
        d_gate = (d_act * up * sigmoid * (1.0 + gate * (1.0 - sigmoid))).astype(LOW)
        d_up = (d_act * silu).astype(LOW)
        columns = pl.ds(pl.multiple_of(step * TILE, TILE), TILE)
        active_ref[...] = (silu * up).astype(LOW)
        d_gate_ref[...] = d_gate
        d_up_ref[...] = d_up
        d_gate_all[:, columns] = d_gate
        d_up_all[:, columns] = d_up

    @pl.when(step >= tiles)
    def _():
        store_blocks(
            out_refs,
            dot_nt(d_gate_all[...], gate_rows_ref[...]) + dot_nt(d_up_all[...], up_rows_ref[...]),
        )


def ffn_both(x_blocks, g_rows, weights):
    blocks = len(x_blocks)
    rows, width = x_blocks[0].shape
    tokens = g_rows.shape[0]
    units = weights.shape[1] // 3
    tiles = units // TILE

    def columns(part):
        return pl.BlockSpec(
            (width, TILE), lambda j: (0, jnp.minimum(j, tiles - 1) + part * tiles)
        )

    def weight_rows(part):
        return pl.BlockSpec((TILE, units), lambda j: (jnp.maximum(j - tiles, 0), part))

    outs = tile_call(
        functools.partial(ffn_both_kernel, blocks, tiles),
        "ffn_both",
        tiles + width // TILE,
        [whole((rows, width))] * blocks
        + [whole((tokens, width)), columns(0), columns(1), columns(2)]
        + [weight_rows(0), weight_rows(1)],
        [pl.BlockSpec((tokens, TILE), lambda j: (0, jnp.minimum(j, tiles - 1)))] * 3
        + [pl.BlockSpec((rows, TILE), lambda j: (0, jnp.maximum(j - tiles, 0)))] * blocks,
        [jax.ShapeDtypeStruct((tokens, units), LOW)] * 3 + block_shapes(blocks, rows, width),
        10 * tokens * width * units,
        [pltpu.VMEM((tokens, width), LOW)] + [pltpu.VMEM((tokens, units), LOW)] * 2,
    )(*x_blocks, g_rows, *([weights] * 5))
    return outs[0], outs[1], outs[2], outs[3:]


def ffn_out_kernel(active_ref, down_ref, *out_refs):
    store_blocks(out_refs, dot_nt(active_ref[...], down_ref[...]))


def ffn_out(blocks, active, weights, *deps):
    tokens, units = active.shape
    width = weights.shape[0]
    rows = tokens // blocks
    return tile_call(
        ffn_out_kernel,
        "ffn_out",
        width // TILE,
        [whole((tokens, units)), pl.BlockSpec((TILE, units), lambda j: (j, 2))],
        [pl.BlockSpec((rows, TILE), lambda j: (0, j))] * blocks,
        block_shapes(blocks, rows, width),
        2 * tokens * width * units,
        deps=len(deps),
    )(active, weights, *deps)


def ffn_grads_kernel(blocks, *refs):
    x_refs = refs[:blocks]
    g_ref, active_ref, d_gate_ref, d_up_ref, grads_ref, mark_ref = refs[blocks:]
    mark_ref[...] = jnp.zeros_like(mark_ref)
    units = active_ref.shape[1]
    x_turned = jnp.concatenate([x_ref[...] for x_ref in x_refs], axis=0).T
    grads_ref[:, :units] = dot_nn(x_turned, d_gate_ref[...]).astype(LOW)
    grads_ref[:, units : 2 * units] = dot_nn(x_turned, d_up_ref[...]).astype(LOW)
    grads_ref[:, 2 * units :] = dot_nn(g_ref[...].T, active_ref[...]).astype(LOW)


def ffn_grads(x_blocks, g_rows, active, d_gate, d_up, *deps):
    blocks = len(x_blocks)
    rows, width = x_blocks[0].shape
    tokens, units = active.shape
    return tile_call(
        functools.partial(ffn_grads_kernel, blocks),
        "ffn_grads",
        width // TILE,
        [pl.BlockSpec((rows, TILE), lambda j: (0, j))] * blocks
        + [pl.BlockSpec((tokens, TILE), lambda j: (0, j))]
        + [whole((tokens, units))] * 3,
        [pl.BlockSpec((TILE, 3 * units), lambda j: (j, 0)), whole((8, 128))],
        [
            jax.ShapeDtypeStruct((width, 3 * units), LOW),
            jax.ShapeDtypeStruct((8, 128), F32),
        ],
        6 * tokens * width * units,
        deps=len(deps),
    )(*x_blocks, g_rows, active, d_gate, d_up, *deps)


def row_grads_kernel(blocks, turned, adds, order_ref, *refs):
    left_refs = refs[:blocks]
    right_ref = refs[blocks]
    left = jnp.concatenate([left_ref[...] for left_ref in left_refs], axis=0).T
    dot = dot_nt if turned else dot_nn
    grad = dot(left, right_ref[...])
    if adds:
        got_ref, kept_ref, sent_ref = refs[blocks + 1 :]
        grad = grad + got_ref[0].astype(F32)

        @pl.when(pl.program_id(0) < 2)
        def _():
            kept_ref[0] = grad

        @pl.when(pl.program_id(0) >= 2)
        def _():
            sent_ref[0] = grad.astype(LOW)

        return
    refs[blocks + 1][0] = grad.astype(LOW)


def row_grads(left_blocks, right, turned, order, got, name, *deps):
    blocks = len(left_blocks)
    rows = left_blocks[0].shape[0]
    columns = right.shape[0] if turned else right.shape[1]
    size = left_blocks[0].shape[1] // 8
    block = pl.BlockSpec((1, size, columns), lambda j, o: (j, 0, 0))
    in_specs = [pl.BlockSpec((rows, size), lambda j, o: (0, o[j]))] * blocks + [
        pl.BlockSpec(right.shape, lambda j, o: (0, 0))
    ]
    inputs = [*left_blocks, right]
    if got is None:
        out_specs = [block]
        out_shape = [jax.ShapeDtypeStruct((4, size, columns), LOW)]
    else:
        in_specs.append(block)
        inputs.append(got)
        out_specs = [
            pl.BlockSpec((1, size, columns), lambda j, o: (jnp.minimum(j, 1), 0, 0)),
            pl.BlockSpec((1, size, columns), lambda j, o: (jnp.maximum(j, 2) - 2, 0, 0)),
        ]
        out_shape = [
            jax.ShapeDtypeStruct((2, size, columns), F32),
            jax.ShapeDtypeStruct((2, size, columns), LOW),
        ]
    kernel = functools.partial(row_grads_kernel, blocks, turned, got is not None)
    kernel = with_deps(kernel, len(inputs), len(deps), 1)
    in_specs += [pl.BlockSpec(memory_space=pl.ANY)] * len(deps)
    return pl.pallas_call(
        kernel,
        grid_spec=pltpu.PrefetchScalarGridSpec(
            num_scalar_prefetch=1, grid=(4,), in_specs=in_specs, out_specs=out_specs
        ),
        out_shape=out_shape,
        compiler_params=pltpu.CompilerParams(
            dimension_semantics=("arbitrary",), vmem_limit_bytes=VMEM_LIMIT
        ),
        cost_estimate=SMALL_COST,
        name=name,
    )(order, *inputs, *deps)


def project_back_kernel(blocks, groups, terms, peer_ref, *refs):
    q_refs, refs = refs[:groups], refs[groups:]
    term_refs, refs = refs[:terms], refs[terms:]
    cos_ref, sin_ref, w_ref = refs[:3]
    out_refs = refs[3 : 3 + blocks]
    d_projected_ref, turned, placed = refs[3 + blocks :]
    heads = q_refs[0].shape[0]
    rows = out_refs[0].shape[0]
    half = HD // 2

    @pl.when(pl.program_id(0) == 0)
    def _():
        for group in range(groups):
            d_projected_ref[group * heads : (group + 1) * heads] = q_refs[group][...]
            part = pl.ds(group * 2 * HD, 2 * HD)
            total = term_refs[0][part, :].astype(F32)
            for term_ref in term_refs[1:]:
                total = total + term_ref[part, :].astype(F32)
            first, second = total[:half], total[half:HD]
            key = groups * heads + group * HD
            d_projected_ref[key : key + half] = (
                first * cos_ref[...] + second * sin_ref[...]
            ).astype(LOW)
            d_projected_ref[key + half : key + HD] = (
                second * cos_ref[...] - first * sin_ref[...]
            ).astype(LOW)
            d_projected_ref[key + groups * HD : key + (groups + 1) * HD] = total[HD:].astype(LOW)
        turned[...] = d_projected_ref[...].T
        for block in range(blocks):
            start = pl.multiple_of(peer_ref[block] * rows, rows)
            placed[block * rows : (block + 1) * rows] = turned[pl.ds(start, rows)]

    store_blocks(out_refs, dot_nt(placed[...], w_ref[...]))


def project_back(peers, d_query, kv_terms, cosine, sine, weights, *deps):
    blocks, groups, terms = peers.shape[0], len(d_query), len(kv_terms)
    heads, tokens = d_query[0].shape
    columns = groups * (heads + 2 * HD)
    width = weights.shape[0]
    rows = tokens // blocks
    inputs = [*d_query, *kv_terms, cosine, sine]
    outs = pl.pallas_call(
        with_deps(
            functools.partial(project_back_kernel, blocks, groups, terms),
            len(inputs) + 1,
            len(deps),
            1,
        ),
        grid_spec=pltpu.PrefetchScalarGridSpec(
            num_scalar_prefetch=1,
            grid=(width // TILE,),
            in_specs=[pl.BlockSpec(each.shape, lambda j, o: (0, 0)) for each in inputs]
            + [pl.BlockSpec((TILE, columns), lambda j, o: (j, 0))]
            + [pl.BlockSpec(memory_space=pl.ANY)] * len(deps),
            out_specs=[pl.BlockSpec((rows, TILE), lambda j, o: (0, j))] * blocks
            + [pl.BlockSpec((columns, tokens), lambda j, o: (0, 0))],
            scratch_shapes=[
                pltpu.VMEM((tokens, columns), LOW),
                pltpu.VMEM((tokens, columns), LOW),
            ],
        ),
        out_shape=block_shapes(blocks, rows, width)
        + [jax.ShapeDtypeStruct((columns, tokens), LOW)],
        compiler_params=pltpu.CompilerParams(
            dimension_semantics=("arbitrary",), vmem_limit_bytes=VMEM_LIMIT
        ),
        cost_estimate=SMALL_COST,
        name="project_back",
    )(peers, *inputs, weights, *deps)
    return outs[:blocks], outs[blocks]


def place_rows_kernel(blocks, peer_ref, *refs):
    out_ref = refs[blocks]
    for block in range(blocks):

        @pl.when(pl.program_id(0) == block)
        def _(block=block):
            out_ref[...] = refs[block][...].astype(out_ref.dtype)


def place_rows(peers, blocks, dtype, *deps):
    count = len(blocks)
    rows, width = blocks[0].shape
    return pl.pallas_call(
        with_deps(functools.partial(place_rows_kernel, count), count, len(deps), 1),
        grid_spec=pltpu.PrefetchScalarGridSpec(
            num_scalar_prefetch=1,
            grid=(count,),
            in_specs=[pl.BlockSpec((rows, width), lambda j, o: (0, 0))] * count
            + [pl.BlockSpec(memory_space=pl.ANY)] * len(deps),
            out_specs=pl.BlockSpec((rows, width), lambda j, o: (o[j], 0)),
        ),
        out_shape=jax.ShapeDtypeStruct((count * rows, width), dtype),
        compiler_params=pltpu.CompilerParams(
            dimension_semantics=("arbitrary",), vmem_limit_bytes=VMEM_LIMIT
        ),
        cost_estimate=SMALL_COST,
        name="place_rows",
    )(peers, *blocks, *deps)


def project_out_kernel(blocks, parts, peer_ref, attn_ref, *refs):
    w_refs, out_refs = refs[:parts], refs[parts : parts + blocks]
    placed_ref, turned = refs[parts + blocks :]
    rows = out_refs[0].shape[0]

    @pl.when(pl.program_id(0) == 0)
    def _():
        turned[...] = attn_ref[...].T
        for block in range(blocks):
            start = pl.multiple_of(peer_ref[block] * rows, rows)
            placed_ref[block * rows : (block + 1) * rows] = turned[pl.ds(start, rows)]

    weights = jnp.concatenate([w_ref[...] for w_ref in w_refs], axis=1)
    store_blocks(out_refs, dot_nt(placed_ref[...], weights))


def project_out(peers, attn_in, weights, start):
    blocks = peers.shape[0]
    columns, tokens = attn_in.shape
    width = weights.shape[0]
    rows = tokens // blocks
    size = math.gcd(start, columns)
    parts = columns // size

    def part_spec(part):
        return pl.BlockSpec((TILE, size), lambda j, o: (j, start // size + part))

    outs = pl.pallas_call(
        functools.partial(project_out_kernel, blocks, parts),
        grid_spec=pltpu.PrefetchScalarGridSpec(
            num_scalar_prefetch=1,
            grid=(width // TILE,),
            in_specs=[pl.BlockSpec((columns, tokens), lambda j, o: (0, 0))]
            + [part_spec(part) for part in range(parts)],
            out_specs=[pl.BlockSpec((rows, TILE), lambda j, o: (0, j))] * blocks
            + [pl.BlockSpec((tokens, columns), lambda j, o: (0, 0))],
            scratch_shapes=[pltpu.VMEM((tokens, columns), LOW)],
        ),
        out_shape=block_shapes(blocks, rows, width)
        + [jax.ShapeDtypeStruct((tokens, columns), LOW)],
        compiler_params=pltpu.CompilerParams(
            dimension_semantics=("arbitrary",), vmem_limit_bytes=VMEM_LIMIT
        ),
        cost_estimate=pl.CostEstimate(
            flops=3 * tokens * columns * width,
            bytes_accessed=4 * width * columns,
            transcendentals=0,
        ),
        name="project_out",
    )(peers, attn_in, *([weights] * parts))
    return outs[:blocks], outs[blocks]


def mix_back_kernel(blocks, parts, peer_ref, *refs):
    mid_refs, w_refs = refs[:blocks], refs[blocks : blocks + parts]
    out_ref, summed, placed = refs[blocks + parts :]
    rows = mid_refs[0].shape[0]
    mid = jnp.concatenate([mid_ref[...] for mid_ref in mid_refs], axis=0)
    weights = jnp.concatenate([w_ref[...] for w_ref in w_refs], axis=1)
    product = dot_nn(mid, weights)

    @pl.when(pl.program_id(0) == 0)
    def _():
        summed[...] = product

    @pl.when(pl.program_id(0) > 0)
    def _():
        summed[...] += product

    @pl.when(pl.program_id(0) == pl.num_programs(0) - 1)
    def _():
        for block in range(blocks):
            start = pl.multiple_of(peer_ref[block] * rows, rows)
            placed[pl.ds(start, rows)] = summed[block * rows : (block + 1) * rows].astype(LOW)
        out_ref[...] = placed[...].T


def mix_back(peers, mid_blocks, weights, start, columns):
    blocks = len(mid_blocks)
    rows, width = mid_blocks[0].shape
    tokens = rows * blocks
    depth = 2 * TILE
    size = math.gcd(start, columns)
    parts = columns // size

    def part_spec(part):
        return pl.BlockSpec((depth, size), lambda j, o: (j, start // size + part))

    return pl.pallas_call(
        functools.partial(mix_back_kernel, blocks, parts),
        grid_spec=pltpu.PrefetchScalarGridSpec(
            num_scalar_prefetch=1,
            grid=(width // depth,),
            in_specs=[pl.BlockSpec((rows, depth), lambda j, o: (0, j))] * blocks
            + [part_spec(part) for part in range(parts)],
            out_specs=pl.BlockSpec((columns, tokens), lambda j, o: (0, 0)),
            scratch_shapes=[pltpu.VMEM((tokens, columns), F32), pltpu.VMEM((tokens, columns), LOW)],
        ),
        out_shape=jax.ShapeDtypeStruct((columns, tokens), LOW),
        compiler_params=pltpu.CompilerParams(
            dimension_semantics=("arbitrary",), vmem_limit_bytes=VMEM_LIMIT
        ),
        cost_estimate=pl.CostEstimate(
            flops=3 * tokens * columns * width,
            bytes_accessed=4 * width * columns,
            transcendentals=0,
        ),
        name="mix_back",
    )(peers, *mid_blocks, *([weights] * parts))


def is_square():
    return lax.axis_size("dp") == 2 and lax.axis_size("ctx") == 4


def swap_core(values):
    return lax.ppermute(values, "ctx", flip_pairs(4, 1))


def swap_across(values):
    return lax.ppermute(values, "ctx", flip_pairs(4, 2))


def swap_along(values):
    return lax.ppermute(values, "dp", flip_pairs(2, 1))


def owner_order(core_flip, across_first):
    along, ctx = lax.axis_index("dp"), lax.axis_index("ctx")
    order = []
    for block in range(4):
        high, low = block >> 1, block & 1
        flip_x, flip_y = (high, low) if across_first else (low, high)
        order.append(((along ^ flip_y) << 2) | (ctx ^ (flip_x << 1) ^ core_flip))
    return jnp.stack(order).astype(jnp.int32)


def travel_open(left_blocks, right, turned, across_first, name, *deps):
    far = row_grads(
        left_blocks, right, turned, owner_order(1, across_first), None, name + "_far", *deps
    )[0]
    return swap_core(far)


def travel_cross(left_blocks, right, turned, across_first, got, name, *deps):
    kept, sent = row_grads(
        left_blocks, right, turned, owner_order(0, across_first), got, name + "_near", *deps
    )
    swap = swap_across if across_first else swap_along
    return kept, swap(sent)


def travel_last(kept, got, across_first):
    swap = swap_along if across_first else swap_across
    total = kept + got.astype(F32)
    return [total[0], swap(total[1].astype(LOW))]


def small_grads_kernel(one_ref, mid_ref, d_projected_ref, attn_ref, grads_ref):
    split = d_projected_ref.shape[0]
    grads_ref[:, :split] = dot_nt(one_ref[...].T, d_projected_ref[...]).astype(LOW)
    grads_ref[:, split:] = dot_nn(mid_ref[...].T, attn_ref[...]).astype(LOW)


def small_grads(normed_one, d_mid_low, d_projected, attn_in):
    tokens, width = normed_one.shape
    columns = d_projected.shape[0] + attn_in.shape[1]
    return tile_call(
        small_grads_kernel,
        "small_grads",
        width // TILE,
        [pl.BlockSpec((tokens, TILE), lambda j: (0, j))] * 2
        + [whole(d_projected.shape), whole(attn_in.shape)],
        [pl.BlockSpec((TILE, columns), lambda j: (j, 0))],
        [jax.ShapeDtypeStruct((width, columns), LOW)],
        2 * tokens * width * columns,
    )(normed_one, d_mid_low, d_projected, attn_in)[0]


def adamw_kernel(turned, step_rate, w_ref, first_ref, second_ref, *refs):
    grad_refs, out_refs, mark_ref = refs[:-4], refs[-4:-1], refs[-1]
    mark_ref[...] = jnp.zeros_like(mark_ref)
    gradient = grad_refs[0][...].astype(F32)
    for grad_ref in grad_refs[1:]:
        gradient = gradient + grad_ref[...].astype(F32)
    if turned:
        gradient = gradient.T
    results = adamw_step(
        w_ref[...], first_ref[...], second_ref[...], gradient, step_rate, WEIGHT_DECAY
    )
    for out_ref, result in zip(out_refs, results):
        out_ref[...] = result


def adamw_call(weight, first, second, terms, start, turned, step_rate, name, *deps):
    rows, columns = weight.shape
    long = rows if turned else columns
    size = math.gcd(math.gcd(start, long), 512)
    if turned:
        spec = pl.BlockSpec((size, columns), lambda j: (j, 0))
    else:
        spec = pl.BlockSpec((rows, size), lambda j: (0, j))
    grad_specs = [
        pl.BlockSpec((term.shape[0], size), lambda j: (0, j + start // size)) for term in terms
    ]
    return tile_call(
        functools.partial(adamw_kernel, turned, step_rate),
        name,
        long // size,
        [spec, spec, spec] + grad_specs,
        [spec] * 3 + [whole((8, 128))],
        [jax.ShapeDtypeStruct(weight.shape, F32)] * 3 + [jax.ShapeDtypeStruct((8, 128), F32)],
        20 * weight.size,
        deps=len(deps),
    )(weight, first, second, *terms, *deps)


def local(
    hidden_in,
    positions,
    cotangent,
    w_qkv,
    w_qkv_first,
    w_qkv_second,
    w_out,
    w_out_first,
    w_out_second,
    w_gate_up,
    w_gate_up_first,
    w_gate_up_second,
    w_down,
    w_down_first,
    w_down_second,
    norm_gains,
    norm_gains_first,
    norm_gains_second,
):
    tensor_count = lax.axis_size("tensor")
    tensor_here = lax.axis_index("tensor")
    ctx_here = lax.axis_index("ctx")
    heads_here = HQ // tensor_count
    kv_here = KV // tensor_count
    head_ratio = HQ // KV
    units_here = FF // tensor_count
    q_cols = heads_here * HD
    k_cols = kv_here * HD
    tok_rows = hidden_in.shape[1]
    seq_rows = positions.shape[1]
    own_rows = tok_rows // tensor_count
    place_row = positions[0]
    query_places = lax.dynamic_slice_in_dim(place_row, ctx_here * tok_rows, tok_rows)
    run_ranks = place_row[::RUN] // RUN
    runs = seq_rows // RUN
    order = jnp.sum(
        jnp.where(
            run_ranks[None, :] == jnp.arange(runs, dtype=jnp.int32)[:, None],
            jnp.arange(runs, dtype=jnp.int32)[None, :],
            0,
        ),
        axis=1,
    ).astype(jnp.int32)
    query_ranks = query_places[::RUN] // RUN

    small_shard = jnp.concatenate([w_qkv.astype(LOW), w_out.astype(LOW).T], axis=1)
    full_small = lax.all_gather(small_shard, ("dp", "ctx"), axis=0, tiled=True)
    full_qkv = full_small[:, : q_cols + 2 * k_cols]
    ffn_shard = jnp.concatenate([w_gate_up.astype(LOW), w_down.astype(LOW).T], axis=1)
    full_ffn = lax.all_gather(ffn_shard, ("dp", "ctx"), axis=0, tiled=True)
    stacked = spread(spread(norm_gains.astype(LOW).astype(F32)[None], "ctx"), "dp")
    gain_values = jnp.swapaxes(stacked, 0, 1).reshape(norm_gains.shape[0], -1)

    hidden = hidden_in[0]
    grad_top = cotangent[0]
    own_start = tensor_here * own_rows
    hidden_own = lax.dynamic_slice_in_dim(hidden, own_start, own_rows).astype(F32)
    grad_own = lax.dynamic_slice_in_dim(grad_top, own_start, own_rows).astype(F32)

    x_hat_one, factor_one = normalize(hidden.astype(F32))
    normed_one = (x_hat_one * gain_values[0]).astype(LOW)
    projected = contract(full_qkv, normed_one, 0, 1)
    cosine, sine = rotary_tables(query_places)
    queries = (
        rotate(projected[:q_cols].reshape(kv_here, head_ratio, HD, tok_rows), cosine, sine)
        * SCORE_SCALE
    ).astype(LOW)
    keys_here = rotate(
        projected[q_cols : q_cols + k_cols].reshape(kv_here, HD, tok_rows), cosine, sine
    ).astype(LOW)
    values_here = projected[q_cols + k_cols :].reshape(kv_here, HD, tok_rows).astype(LOW)
    kv_local = jnp.concatenate([keys_here, values_here], axis=1)
    ctx_peers, tensor_peers = axis_peers("ctx"), axis_peers("tensor")
    kv_blocks = gather_blocks(kv_local, "ctx")
    mixed, attn_low, log_total = attend_forward(order, query_ranks, ctx_peers, queries, kv_blocks)

    def from_here(values, axis=0):
        return blocks_from_here(tensor_count, tensor_here, own_rows, values, axis)

    grad_top = from_here(grad_top)
    out_start = q_cols + 2 * k_cols
    out_parts, attn_in = project_out(
        tensor_peers, attn_low.reshape(q_cols, tok_rows), full_small, out_start
    )
    middle = hidden_own + sum_scatter(out_parts, "tensor")
    x_hat_two, factor_two = normalize(middle)
    normed_two = gather_blocks((x_hat_two * gain_values[1]).astype(LOW), "tensor")
    active, d_gate, d_up, d_two_parts = ffn_both(normed_two, grad_top, full_ffn)
    d_two_pieces = scatter_begin(d_two_parts, "tensor")
    ffn_parts = list(ffn_out(tensor_count, active, full_ffn, d_two_parts[0]))
    d_two_pieces[2], ffn_parts[0] = lax.optimization_barrier((d_two_pieces[2], ffn_parts[0]))
    d_two_pieces = scatter_middle(d_two_pieces, "tensor")
    grad_ffn, mark = ffn_grads(normed_two, grad_top, active, d_gate, d_up, ffn_parts[0])
    d_two_pieces[1:], mark = lax.optimization_barrier((d_two_pieces[1:], mark))
    grad_ffn = held_until(grad_ffn, d_two_pieces[-1])
    red_ffn = lax.optimization_barrier(
        lax.psum_scatter(grad_ffn, ("dp", "ctx"), scatter_dimension=0, tiled=True)
    )
    d_normed_two = scatter_end(d_two_pieces)

    grad_gain_two = jnp.sum(d_normed_two * x_hat_two, axis=0)
    d_middle = grad_own + norm_back(d_normed_two * gain_values[1], x_hat_two, factor_two)
    d_mid_blocks = gather_blocks(d_middle.astype(LOW), "tensor")
    d_mixed = mix_back(tensor_peers, d_mid_blocks, full_small, out_start, q_cols).reshape(
        kv_here, head_ratio, HD, tok_rows
    )
    mark, ffn_parts = lax.optimization_barrier((d_mid_blocks[3:], ffn_parts))
    ffn_pieces = scatter_begin(ffn_parts, "tensor")
    d_query, kv_terms = [], []
    for group in range(kv_here):
        d_heads, *kv_terms = attend_backward(
            group, order, query_ranks, ctx_peers, kv_blocks, kv_terms, queries, d_mixed, mixed,
            log_total, cosine, sine, *mark,
        )
        if group == 0:
            kv_terms, ffn_pieces[1:3] = lax.optimization_barrier((kv_terms, ffn_pieces[1:3]))
            ffn_pieces = scatter_middle(ffn_pieces, "tensor")
        d_query.append(d_heads.reshape(-1, tok_rows))
    kv_terms, ffn_pieces = lax.optimization_barrier((kv_terms, ffn_pieces))
    kv_pieces = scatter_begin(kv_terms, "ctx")
    if is_square():
        out_got = travel_open(d_mid_blocks, attn_in, False, True, "grads_out", kv_terms[0])
    block_own = (middle + scatter_end(ffn_pieces)).astype(LOW)
    if tensor_count == 4:
        block_far = lax.ppermute(block_own, "tensor", flip_pairs(4, 2))
        block_near = lax.ppermute(block_own, "tensor", flip_pairs(4, 1))
    else:
        block_blocks = gather_blocks(block_own, "tensor")

    kv_pieces = scatter_middle(kv_pieces, "ctx")
    if tensor_count == 4:
        kv_pieces[-1], block_far, block_near = lax.optimization_barrier(
            (kv_pieces[-1], block_far, block_near)
        )
    d_one_parts, d_projected = project_back(
        tensor_peers, d_query, kv_pieces, cosine, sine, full_small
    )
    d_one_pieces = scatter_begin(d_one_parts, "tensor")
    adamw_down = functools.partial(
        adamw_call, w_down, w_down_first, w_down_second, [red_ffn], 2 * units_here, True,
        LEARN_RATE, "adamw_down",
    )
    adamw_gate_up = functools.partial(
        adamw_call, w_gate_up, w_gate_up_first, w_gate_up_second, [red_ffn], 0, False,
        LEARN_RATE, "adamw_gate_up",
    )
    if is_square():
        out_kept, out_got = travel_cross(
            d_mid_blocks, attn_in, False, True, out_got, "grads_out", d_one_parts[0]
        )
        d_one_pieces[2], out_kept = lax.optimization_barrier((d_one_pieces[2], out_kept))
        d_one_pieces = scatter_middle(d_one_pieces, "tensor")
        qkv_far = row_grads(
            [normed_one], d_projected, True, owner_order(1, False), None, "grads_qkv_far", out_kept
        )[0]
        d_one_pieces[1:], out_kept, qkv_far = lax.optimization_barrier(
            (d_one_pieces[1:], out_kept, qkv_far)
        )
        qkv_got = swap_core(qkv_far)
    else:
        grad_small = small_grads(
            normed_one, jnp.concatenate(d_mid_blocks, axis=0), d_projected, attn_in
        )
        d_one_pieces = scatter_middle(d_one_pieces, "tensor")
        red_small = lax.optimization_barrier(
            lax.psum_scatter(grad_small, ("dp", "ctx"), scatter_dimension=0, tiled=True)
        )
    d_normed_one = scatter_end(d_one_pieces)
    x_hat_own, factor_own = normalize(hidden_own)
    grad_gain_one = jnp.sum(d_normed_one * x_hat_own, axis=0)
    grad_in_own = d_middle + norm_back(d_normed_one * gain_values[0], x_hat_own, factor_own)
    grad_in_low = grad_in_own.astype(LOW)
    gain_rows = jnp.stack([grad_gain_one, grad_gain_two])
    if is_square():
        qkv_kept, qkv_got = travel_cross(
            [normed_one], d_projected, True, False, qkv_got, "grads_qkv"
        )
    gu_first, gu_second, gu_new, mark = adamw_gate_up(d_normed_one)
    if tensor_count == 4:
        near = lax.ppermute(grad_in_low, "tensor", flip_pairs(4, 1))
        far = lax.ppermute(grad_in_low, "tensor", flip_pairs(4, 2))
        near, far, mark, gain_rows, block_far = lax.optimization_barrier(
            (near, far, mark, gain_rows, block_far)
        )
        if is_square():
            near, out_got, qkv_kept = lax.optimization_barrier((near, out_got, qkv_kept))
        grad_in_blocks = [grad_in_low, near, far, lax.ppermute(far, "tensor", flip_pairs(4, 1))]
        block_last = lax.ppermute(block_far, "tensor", flip_pairs(4, 1))
        block_blocks = [block_own, block_near, block_far, block_last]
    else:
        grad_in_blocks = gather_blocks(grad_in_low, "tensor")
    small_start = 0
    if not is_square():
        small_start, out_terms, qkv_terms = out_start, [red_small], [red_small]
    else:
        out_terms = travel_last(out_kept, out_got, True)
        qkv_terms = travel_last(qkv_kept, qkv_got, False)
    down_first, down_second, down_new, mark = adamw_down(mark)
    out_first, out_second, out_new, mark = adamw_call(
        w_out, w_out_first, w_out_second, out_terms, small_start, True, OUT_RATE, "adamw_out", mark
    )
    gain_sums = sum_everywhere(gain_rows, "tensor")
    gain_parts = jnp.swapaxes(gain_sums.reshape(2, -1, norm_gains.shape[1]), 0, 1)
    red_gains = gains_scatter(gains_scatter(gain_parts, "dp"), "ctx")[0]
    grad_in_blocks[3], red_gains = lax.optimization_barrier((grad_in_blocks[3], red_gains))
    qkv_first, qkv_second, qkv_new, last_mark = adamw_call(
        w_qkv, w_qkv_first, w_qkv_second, qkv_terms, 0, False, LEARN_RATE, "adamw_qkv", mark
    )
    grad_in = place_rows(tensor_peers, grad_in_blocks, F32, block_blocks[3], mark)
    grad_in = grad_in.reshape(hidden_in.shape)
    block_out = place_rows(tensor_peers, block_blocks, LOW).reshape(hidden_in.shape)
    gain_first, gain_second, gain_new = adamw_step(
        norm_gains, norm_gains_first, norm_gains_second, red_gains, GAIN_RATE, 0.0
    )
    return (
        block_out,
        grad_in,
        qkv_first,
        qkv_second,
        qkv_new,
        out_first,
        out_second,
        out_new,
        gu_first,
        gu_second,
        gu_new,
        down_first,
        down_second,
        down_new,
        gain_first,
        gain_second,
        gain_new,
    )


def solution(mesh):
    tokens = P("dp", "ctx", None)
    rows = P(("dp", "ctx"), "tensor")
    columns = P("tensor", ("dp", "ctx"))
    gains = P(None, ("dp", "ctx"))
    placed = (
        (tokens, P("dp", None), tokens)
        + (rows,) * 3
        + (columns,) * 3
        + (rows,) * 3
        + (columns,) * 3
        + (gains,) * 3
    )
    return jax.shard_map(
        local,
        mesh=mesh,
        in_specs=placed,
        out_specs=(tokens, tokens) + placed[3:],
        check_vma=False,
    )
```

```python
import functools
import math

import jax
import jax.numpy as jnp
from jax import lax
from jax.experimental import pallas as pl
from jax.experimental.pallas import tpu as pltpu
from jax.sharding import PartitionSpec as P

HQ = 32
KV = 8
HD = 64
FF = 8192
STEP = 10
RUN = 256


NORM_EPS = 1e-05
ROPE_THETA = 500000.0
SCORE_SCALE = 0.125
LEARN_RATE = 0.01
OUT_RATE = 0.05
GAIN_RATE = 0.25
BETA_ONE = 0.9
BETA_TWO = 0.95
ADAM_EPS = 1e-08
WEIGHT_DECAY = 0.1

F32 = jnp.float32
LOW = jnp.bfloat16


def contract(left, right, left_dim, right_dim):
    return lax.dot_general(
        left, right, (((left_dim,), (right_dim,)), ((), ())), preferred_element_type=F32
    )


def rotary_tables(places):
    half = HD // 2
    freqs = ROPE_THETA ** (-(jnp.arange(half, dtype=F32) * 2.0 / HD))
    angles = freqs[:, None] * places.astype(F32)[None, :]
    return jnp.cos(angles), jnp.sin(angles)


def rotate(vectors, cosine, sine):
    half = HD // 2
    first = vectors[..., :half, :]
    second = vectors[..., half:, :]
    return jnp.concatenate(
        [first * cosine - second * sine, second * cosine + first * sine], axis=-2
    )


def normalize(values):
    factor = lax.rsqrt(jnp.mean(values * values, axis=-1, keepdims=True) + NORM_EPS)
    return (values * factor, factor)


def norm_back(grad_hat, x_hat, factor):
    return factor * (grad_hat - x_hat * jnp.mean(grad_hat * x_hat, axis=-1, keepdims=True))


def adamw_step(weight, first, second, gradient, step_rate, decay_rate):
    first_new = BETA_ONE * first + (1.0 - BETA_ONE) * gradient
    second_new = BETA_TWO * second + (1.0 - BETA_TWO) * gradient * gradient
    first_hat = first_new / (1.0 - BETA_ONE**STEP)
    second_hat = second_new / (1.0 - BETA_TWO**STEP)
    weight_new = weight - step_rate * (
        first_hat / (jnp.sqrt(second_hat) + ADAM_EPS) + decay_rate * weight
    )
    return (first_new, second_new, weight_new)


def shift_pairs(count, step):
    return [(i, (i + step) % count) for i in range(count)]


def flip_pairs(count, mask):
    return [(i, i ^ mask) for i in range(count)]


def cut(parts, index, rows):
    return lax.dynamic_slice_in_dim(parts, index * rows, rows)


def scatter_begin(parts, axis):
    count = lax.axis_size(axis)
    blocks = parts
    if not isinstance(parts, (list, tuple)):
        rows = parts.shape[0] // count
        blocks = [parts[step * rows : (step + 1) * rows] for step in range(count)]
    own = blocks[0]
    if count == 4:
        through = lax.ppermute(blocks[3].astype(LOW), axis, flip_pairs(count, 1))
        return [own, blocks[1].astype(LOW), through, blocks[2]]
    return [own] + [
        lax.ppermute(blocks[step].astype(LOW), axis, shift_pairs(count, step))
        for step in range(1, count)
    ]


def scatter_middle(pieces, axis):
    count = lax.axis_size(axis)
    if count == 4:
        own, near, through, far = pieces
        near, through = lax.optimization_barrier((near, through))
        joined = (far.astype(F32) + through.astype(F32)).astype(LOW)
        return [
            own,
            lax.ppermute(near, axis, flip_pairs(count, 1)),
            lax.ppermute(joined, axis, flip_pairs(count, 2)),
        ]
    return pieces


def scatter_end(pieces):
    total = pieces[0].astype(F32)
    for piece in pieces[1:]:
        total = total + piece.astype(F32)
    return total


def sum_scatter(parts, axis):
    return scatter_end(scatter_middle(scatter_begin(parts, axis), axis))


def gains_scatter(parts, axis):
    count = lax.axis_size(axis)
    here = lax.axis_index(axis)
    rows = parts.shape[0] // count
    total = cut(parts, here, rows)
    for step in range(1, count):
        piece = cut(parts, lax.rem(here + step, count), rows)
        total = total + lax.ppermute(piece, axis, shift_pairs(count, step))
    return total


def sum_everywhere(values, axis):
    count = lax.axis_size(axis)
    total = values
    for step in range(1, count):
        total = total + lax.ppermute(values, axis, shift_pairs(count, step))
    return total


def blocks_from_here(count, here, rows, values, axis=0):
    cuts = []
    for step in range(count):
        index = here ^ step if count == 4 else lax.rem(here + step, count)
        cuts.append(lax.dynamic_slice_in_dim(values, index * rows, rows, axis))
    return jnp.concatenate(cuts, axis=axis)


def axis_peers(axis):
    count, here = lax.axis_size(axis), lax.axis_index(axis)
    return jnp.stack(
        [here ^ step if count == 4 else lax.rem(here + step, count) for step in range(count)]
    ).astype(jnp.int32)


def gather_blocks(rows, axis):
    count = lax.axis_size(axis)
    if count == 4:
        near = lax.ppermute(rows, axis, flip_pairs(count, 1))
        far = lax.ppermute(rows, axis, flip_pairs(count, 2))
        near, far = lax.optimization_barrier((near, far))
        last = lax.ppermute(far, axis, flip_pairs(count, 1))
        return [rows, near, far, last]
    return [rows] + [
        lax.ppermute(rows, axis, shift_pairs(count, count - step)) for step in range(1, count)
    ]


def place_blocks(blocks, axis):
    count = lax.axis_size(axis)
    here = lax.axis_index(axis)
    size = blocks[0].shape[0]
    whole_rows = jnp.zeros((count * size,) + blocks[0].shape[1:], blocks[0].dtype)
    for step, block in enumerate(blocks):
        index = here ^ step if count == 4 else lax.rem(here + step, count)
        whole_rows = lax.dynamic_update_slice_in_dim(whole_rows, block, index * size, 0)
    return whole_rows


def spread(rows, axis):
    return place_blocks(gather_blocks(rows, axis), axis)


def block_place(order_ref, rank, per_device):
    run = order_ref[rank]
    return run // per_device, pl.multiple_of((run % per_device) * RUN, RUN)


def dot_nn(left, right):
    return jnp.dot(left, right, preferred_element_type=F32)


def dot_nt(left, right):
    return lax.dot_general(left, right, (((1,), (1,)), ((), ())), preferred_element_type=F32)


def causal_mask(columns):
    keys = lax.broadcasted_iota(jnp.int32, (RUN, columns), 0)
    queries = lax.broadcasted_iota(jnp.int32, (RUN, columns), 1) & (RUN - 1)
    return keys <= queries


def take_blocks(peer_ref, piece_refs, kvn_ref, kvt_ref):
    for block, piece_ref in enumerate(piece_refs):
        kvt_ref[peer_ref[block]] = piece_ref[0]
        kvn_ref[peer_ref[block]] = piece_ref[0].T


def head_columns(head):
    return slice(head * RUN, (head + 1) * RUN)


def forward_kernel(devices, per_device, ratio, order_ref, rank_ref, peer_ref, *refs):
    piece_refs = refs[:devices]
    q_ref, mix_ref, low_ref, lse_ref, q_pad, high, total, summed, kvn_ref, kvt_ref = refs[devices:]
    rank = rank_ref[pl.program_id(1)]

    @pl.when(pl.program_id(1) == 0)
    def _():
        take_blocks(peer_ref, piece_refs, kvn_ref, kvt_ref)

    for head in range(ratio):
        q_pad[:HD, head_columns(head)] = q_ref[0, head]
    q_pad[HD:] = jnp.zeros((HD, ratio * RUN), LOW)

    def visit(step, first):
        device, offset = block_place(order_ref, step, per_device)
        keys = kvn_ref[device, pl.ds(offset, RUN), :]
        values = kvt_ref[device, HD:, pl.ds(offset, RUN)]
        scores = dot_nn(keys, q_pad[...])
        if first:
            scores = jnp.where(causal_mask(ratio * RUN), scores, -1e30)
        top = jnp.max(scores, axis=0, keepdims=True)
        if not first:
            old = high[...]
            top = jnp.maximum(old, top)
            scale = jnp.exp(old - top)
        probs = jnp.exp(scores - top)
        row_sum = jnp.sum(probs, axis=0, keepdims=True)
        product = dot_nn(values, probs.astype(LOW))
        high[...] = top
        if first:
            total[...] = row_sum
            summed[...] = product
        else:
            total[...] = total[...] * scale + row_sum
            summed[...] = summed[...] * scale + product

    visit(rank, True)

    @pl.loop(0, rank)
    def _(step):
        visit(step, False)

    mixed = summed[...] / total[...]
    log_total = high[...] + jnp.log(total[...])
    for head in range(ratio):
        mix_ref[0, head] = mixed[:, head_columns(head)]
        low_ref[0, head] = mixed[:, head_columns(head)].astype(LOW)
        lse_ref[0, head] = log_total[:, head_columns(head)]


def backward_kernel(devices, per_device, ratio, earlier, order_ref, rank_ref, peer_ref, *refs):
    piece_refs, refs = refs[:devices], refs[devices:]
    earlier_refs, refs = refs[:earlier], refs[earlier:]
    q_ref, d_ref, mix_ref, lse_ref, cos_ref, sin_ref, dq_ref = refs[:7]
    dkv_refs = refs[7:-7]
    pads, row_dot, log_total, dq_sum, dkv_sum, kvn_ref, kvt_ref = refs[-7:]
    place = pl.program_id(0)
    rank = rank_ref[place]
    columns = ratio * RUN

    @pl.when(place == 0)
    def _():
        dkv_sum[...] = jnp.zeros_like(dkv_sum)
        take_blocks(peer_ref, piece_refs, kvn_ref, kvt_ref)

    pads[HD:, :columns] = jnp.zeros((HD, columns), LOW)
    pads[:HD, columns:] = jnp.zeros((HD, columns), LOW)
    for head in range(ratio):
        here = head_columns(head)
        pads[:HD, here] = q_ref[0, head]
        pads[HD:, head_columns(ratio + head)] = d_ref[0, head]
        row_dot[:, here] = jnp.sum(
            d_ref[0, head].astype(F32) * mix_ref[0, head], axis=0, keepdims=True
        )
        log_total[:, here] = lse_ref[0, head]

    def visit(step, first):
        device, offset = block_place(order_ref, step, per_device)
        rows = kvn_ref[device, pl.ds(offset, RUN), :]
        keys = kvt_ref[device, :HD, pl.ds(offset, RUN)]
        probs = jnp.exp(dot_nn(rows, pads[:, :columns]) - log_total[...])
        if first:
            probs = jnp.where(causal_mask(columns), probs, 0.0)
        d_probs = dot_nn(rows, pads[:, columns:])
        d_scores = (probs * (d_probs - row_dot[...])).astype(LOW)
        product = dot_nn(keys, d_scores)
        if first:
            dq_sum[...] = product
        else:
            dq_sum[...] += product
        dkv_sum[device, pl.ds(offset, RUN), :] += dot_nt(
            jnp.concatenate([d_scores, probs.astype(LOW)], axis=1), pads[...]
        )

    visit(rank, True)

    @pl.loop(0, rank)
    def _(step):
        visit(step, False)

    half = HD // 2
    for head in range(ratio):
        first = dq_sum[:half, head_columns(head)] * SCORE_SCALE
        second = dq_sum[half:, head_columns(head)] * SCORE_SCALE
        dq_ref[0, head, :half] = (first * cos_ref[...] + second * sin_ref[...]).astype(LOW)
        dq_ref[0, head, half:] = (second * cos_ref[...] - first * sin_ref[...]).astype(LOW)

    @pl.when(place == pl.num_programs(0) - 1)
    def _():
        for block, dkv_ref in enumerate(dkv_refs):
            start = 0
            if earlier:
                start = earlier_refs[block].shape[0]
                dkv_ref[:start] = earlier_refs[block][...]
            dkv_ref[start:] = dkv_sum[peer_ref[block]].T.astype(LOW)


VMEM_LIMIT = 48 * 1024 * 1024
SMALL_COST = pl.CostEstimate(flops=1000, bytes_accessed=1000, transcendentals=0)


def attend_forward(order, ranks, peers, queries, kv_blocks):
    groups, ratio, head_size, tokens = queries.shape
    devices = len(kv_blocks)
    width, per_tokens = kv_blocks[0].shape[1:]
    q_spec = pl.BlockSpec((1, ratio, HD, RUN), lambda g, i, *s: (g, 0, 0, i))
    blocks = groups * (tokens // RUN) * devices * (per_tokens // RUN) * ratio
    return pl.pallas_call(
        functools.partial(forward_kernel, devices, per_tokens // RUN, ratio),
        grid_spec=pltpu.PrefetchScalarGridSpec(
            num_scalar_prefetch=3,
            grid=(groups, tokens // RUN),
            in_specs=[pl.BlockSpec((1, width, per_tokens), lambda g, i, *s: (g, 0, 0))] * devices
            + [q_spec],
            out_specs=[
                q_spec,
                q_spec,
                pl.BlockSpec((1, ratio, 1, RUN), lambda g, i, *s: (g, 0, 0, i)),
            ],
            scratch_shapes=[
                pltpu.VMEM((2 * HD, ratio * RUN), LOW),
                pltpu.VMEM((1, ratio * RUN), F32),
                pltpu.VMEM((1, ratio * RUN), F32),
                pltpu.VMEM((HD, ratio * RUN), F32),
                pltpu.VMEM((devices, per_tokens, width), LOW),
                pltpu.VMEM((devices, width, per_tokens), LOW),
            ],
        ),
        out_shape=[
            jax.ShapeDtypeStruct(queries.shape, F32),
            jax.ShapeDtypeStruct(queries.shape, LOW),
            jax.ShapeDtypeStruct((groups, ratio, 1, tokens), F32),
        ],
        compiler_params=pltpu.CompilerParams(
            dimension_semantics=("arbitrary", "arbitrary"), vmem_limit_bytes=VMEM_LIMIT
        ),
        cost_estimate=pl.CostEstimate(
            flops=blocks * 64 * RUN * RUN * HD,
            bytes_accessed=8 * 1024 * 1024,
            transcendentals=blocks * RUN * RUN,
        ),
        name="attend_forward",
    )(order, ranks, peers, *kv_blocks, queries)


def attend_backward(
    group, order, ranks, peers, kv_blocks, earlier, queries, d_mixed, mixed, log_total, cosine,
    sine, *deps,
):
    groups, ratio, head_size, tokens = queries.shape
    devices = len(kv_blocks)
    width, per_tokens = kv_blocks[0].shape[1:]
    q_spec = pl.BlockSpec((1, ratio, HD, RUN), lambda i, *s: (group, 0, 0, i))
    table = pl.BlockSpec((HD // 2, RUN), lambda i, *s: (0, i))
    blocks = (tokens // RUN) * devices * (per_tokens // RUN) * ratio
    grown = width + (earlier[0].shape[0] if earlier else 0)
    inputs = [*kv_blocks, *earlier, queries, d_mixed, mixed, log_total, cosine, sine]
    return pl.pallas_call(
        with_deps(
            functools.partial(backward_kernel, devices, per_tokens // RUN, ratio, len(earlier)),
            len(inputs),
            len(deps),
            3,
        ),
        grid_spec=pltpu.PrefetchScalarGridSpec(
            num_scalar_prefetch=3,
            grid=(tokens // RUN,),
            in_specs=[pl.BlockSpec((1, width, per_tokens), lambda i, *s: (group, 0, 0))] * devices
            + [pl.BlockSpec(each.shape, lambda i, *s: (0, 0)) for each in earlier]
            + [q_spec] * 3
            + [pl.BlockSpec((1, ratio, 1, RUN), lambda i, *s: (group, 0, 0, i)), table, table]
            + [pl.BlockSpec(memory_space=pl.ANY)] * len(deps),
            out_specs=[pl.BlockSpec((1, ratio, HD, RUN), lambda i, *s: (0, 0, 0, i))]
            + [pl.BlockSpec((grown, per_tokens), lambda i, *s: (0, 0))] * devices,
            scratch_shapes=[
                pltpu.VMEM((2 * HD, 2 * ratio * RUN), LOW),
                pltpu.VMEM((1, ratio * RUN), F32),
                pltpu.VMEM((1, ratio * RUN), F32),
                pltpu.VMEM((HD, ratio * RUN), F32),
                pltpu.VMEM((devices, per_tokens, width), F32),
                pltpu.VMEM((devices, per_tokens, width), LOW),
                pltpu.VMEM((devices, width, per_tokens), LOW),
            ],
        ),
        out_shape=[jax.ShapeDtypeStruct((1,) + queries.shape[1:], LOW)]
        + [jax.ShapeDtypeStruct((grown, per_tokens), LOW)] * devices,
        compiler_params=pltpu.CompilerParams(
            dimension_semantics=("arbitrary",), vmem_limit_bytes=VMEM_LIMIT
        ),
        cost_estimate=pl.CostEstimate(
            flops=blocks * 128 * RUN * RUN * HD,
            bytes_accessed=8 * 1024 * 1024,
            transcendentals=blocks * RUN * RUN,
        ),
        name="attend_backward",
    )(order, ranks, peers, *inputs, *deps)


TILE = 256


def whole(shape):
    return pl.BlockSpec(shape, lambda j: (0,) * len(shape), pipeline_mode=pl.Buffered(1))


def with_deps(kernel, inputs, deps, scalars=0):
    first = scalars + inputs

    def run(*refs):
        kernel(*refs[:first], *refs[first + deps :])

    return run


def tile_call(kernel, name, tiles, in_specs, out_specs, out_shape, flops, scratch=(), deps=0):
    size = sum(math.prod(each.shape) * each.dtype.itemsize for each in out_shape)
    return pl.pallas_call(
        with_deps(kernel, len(in_specs), deps),
        grid=(tiles,),
        in_specs=list(in_specs) + [pl.BlockSpec(memory_space=pl.ANY)] * deps,
        out_specs=out_specs,
        out_shape=out_shape,
        scratch_shapes=scratch,
        compiler_params=pltpu.CompilerParams(
            dimension_semantics=("arbitrary",), vmem_limit_bytes=VMEM_LIMIT
        ),
        cost_estimate=pl.CostEstimate(
            flops=flops * 3 // 2, bytes_accessed=2 * size, transcendentals=0
        ),
        name=name,
    )


def held_until_kernel(values_ref, *refs):
    mark_ref = refs[-1]
    mark_ref[...] = jnp.zeros_like(mark_ref)


def held_until(values, *deps):
    hidden = pl.BlockSpec(memory_space=pl.ANY)
    return pl.pallas_call(
        held_until_kernel,
        in_specs=[hidden] * (1 + len(deps)),
        out_specs=[hidden, pl.BlockSpec(memory_space=pltpu.VMEM)],
        out_shape=[
            jax.ShapeDtypeStruct(values.shape, values.dtype),
            jax.ShapeDtypeStruct((8, 128), F32),
        ],
        input_output_aliases={0: 0},
        name="held_until",
    )(values, *deps)[0]


def store_blocks(out_refs, values):
    rows = out_refs[0].shape[0]
    for block, out_ref in enumerate(out_refs):
        out_ref[...] = values[block * rows : (block + 1) * rows].astype(out_ref.dtype)


def block_shapes(blocks, rows, width):
    kept = (0, 2) if blocks == 4 else (0,)
    return [
        jax.ShapeDtypeStruct((rows, width), F32 if block in kept else LOW)
        for block in range(blocks)
    ]


def ffn_both_kernel(blocks, tiles, *refs):
    x_refs = refs[:blocks]
    g_ref, gate_ref, up_ref, down_ref, gate_rows_ref, up_rows_ref = refs[blocks : blocks + 6]
    active_ref, d_gate_ref, d_up_ref = refs[blocks + 6 : blocks + 9]
    out_refs = refs[blocks + 9 : -3]
    x_all, d_gate_all, d_up_all = refs[-3:]
    step = pl.program_id(0)
    rows = x_refs[0].shape[0]

    @pl.when(step == 0)
    def _():
        for block in range(blocks):
            x_all[block * rows : (block + 1) * rows] = x_refs[block][...]

    @pl.when(step < tiles)
    def _():
        gate = dot_nn(x_all[...], gate_ref[...])
        up = dot_nn(x_all[...], up_ref[...])
        d_act = dot_nn(g_ref[...], down_ref[...])
        sigmoid = 1.0 / (1.0 + jnp.exp(-gate))
        silu = gate * sigmoid
        d_gate = (d_act * up * sigmoid * (1.0 + gate * (1.0 - sigmoid))).astype(LOW)
        d_up = (d_act * silu).astype(LOW)
        columns = pl.ds(pl.multiple_of(step * TILE, TILE), TILE)
        active_ref[...] = (silu * up).astype(LOW)
        d_gate_ref[...] = d_gate
        d_up_ref[...] = d_up
        d_gate_all[:, columns] = d_gate
        d_up_all[:, columns] = d_up

    @pl.when(step >= tiles)
    def _():
        store_blocks(
            out_refs,
            dot_nt(d_gate_all[...], gate_rows_ref[...]) + dot_nt(d_up_all[...], up_rows_ref[...]),
        )


def ffn_both(x_blocks, g_rows, weights):
    blocks = len(x_blocks)
    rows, width = x_blocks[0].shape
    tokens = g_rows.shape[0]
    units = weights.shape[1] // 3
    tiles = units // TILE

    def columns(part):
        return pl.BlockSpec(
            (width, TILE), lambda j: (0, jnp.minimum(j, tiles - 1) + part * tiles)
        )

    def weight_rows(part):
        return pl.BlockSpec((TILE, units), lambda j: (jnp.maximum(j - tiles, 0), part))

    outs = tile_call(
        functools.partial(ffn_both_kernel, blocks, tiles),
        "ffn_both",
        tiles + width // TILE,
        [whole((rows, width))] * blocks
        + [whole((tokens, width)), columns(0), columns(1), columns(2)]
        + [weight_rows(0), weight_rows(1)],
        [pl.BlockSpec((tokens, TILE), lambda j: (0, jnp.minimum(j, tiles - 1)))] * 3
        + [pl.BlockSpec((rows, TILE), lambda j: (0, jnp.maximum(j - tiles, 0)))] * blocks,
        [jax.ShapeDtypeStruct((tokens, units), LOW)] * 3 + block_shapes(blocks, rows, width),
        10 * tokens * width * units,
        [pltpu.VMEM((tokens, width), LOW)] + [pltpu.VMEM((tokens, units), LOW)] * 2,
    )(*x_blocks, g_rows, *([weights] * 5))
    return outs[0], outs[1], outs[2], outs[3:]


def ffn_out_kernel(active_ref, down_ref, *out_refs):
    store_blocks(out_refs, dot_nt(active_ref[...], down_ref[...]))


def ffn_out(blocks, active, weights, *deps):
    tokens, units = active.shape
    width = weights.shape[0]
    rows = tokens // blocks
    return tile_call(
        ffn_out_kernel,
        "ffn_out",
        width // TILE,
        [whole((tokens, units)), pl.BlockSpec((TILE, units), lambda j: (j, 2))],
        [pl.BlockSpec((rows, TILE), lambda j: (0, j))] * blocks,
        block_shapes(blocks, rows, width),
        2 * tokens * width * units,
        deps=len(deps),
    )(active, weights, *deps)


def ffn_grads_kernel(blocks, *refs):
    x_refs = refs[:blocks]
    g_ref, active_ref, d_gate_ref, d_up_ref, grads_ref, mark_ref = refs[blocks:]
    mark_ref[...] = jnp.zeros_like(mark_ref)
    units = active_ref.shape[1]
    x_turned = jnp.concatenate([x_ref[...] for x_ref in x_refs], axis=0).T
    grads_ref[:, :units] = dot_nn(x_turned, d_gate_ref[...]).astype(LOW)
    grads_ref[:, units : 2 * units] = dot_nn(x_turned, d_up_ref[...]).astype(LOW)
    grads_ref[:, 2 * units :] = dot_nn(g_ref[...].T, active_ref[...]).astype(LOW)


def ffn_grads(x_blocks, g_rows, active, d_gate, d_up, *deps):
    blocks = len(x_blocks)
    rows, width = x_blocks[0].shape
    tokens, units = active.shape
    return tile_call(
        functools.partial(ffn_grads_kernel, blocks),
        "ffn_grads",
        width // TILE,
        [pl.BlockSpec((rows, TILE), lambda j: (0, j))] * blocks
        + [pl.BlockSpec((tokens, TILE), lambda j: (0, j))]
        + [whole((tokens, units))] * 3,
        [pl.BlockSpec((TILE, 3 * units), lambda j: (j, 0)), whole((8, 128))],
        [
            jax.ShapeDtypeStruct((width, 3 * units), LOW),
            jax.ShapeDtypeStruct((8, 128), F32),
        ],
        6 * tokens * width * units,
        deps=len(deps),
    )(*x_blocks, g_rows, active, d_gate, d_up, *deps)


def row_grads_kernel(blocks, turned, adds, order_ref, *refs):
    left_refs = refs[:blocks]
    right_ref = refs[blocks]
    left = jnp.concatenate([left_ref[...] for left_ref in left_refs], axis=0).T
    dot = dot_nt if turned else dot_nn
    grad = dot(left, right_ref[...])
    if adds:
        got_ref, kept_ref, sent_ref = refs[blocks + 1 :]
        grad = grad + got_ref[0].astype(F32)

        @pl.when(pl.program_id(0) < 2)
        def _():
            kept_ref[0] = grad

        @pl.when(pl.program_id(0) >= 2)
        def _():
            sent_ref[0] = grad.astype(LOW)

        return
    refs[blocks + 1][0] = grad.astype(LOW)


def row_grads(left_blocks, right, turned, order, got, name, *deps):
    blocks = len(left_blocks)
    rows = left_blocks[0].shape[0]
    columns = right.shape[0] if turned else right.shape[1]
    size = left_blocks[0].shape[1] // 8
    block = pl.BlockSpec((1, size, columns), lambda j, o: (j, 0, 0))
    in_specs = [pl.BlockSpec((rows, size), lambda j, o: (0, o[j]))] * blocks + [
        pl.BlockSpec(right.shape, lambda j, o: (0, 0))
    ]
    inputs = [*left_blocks, right]
    if got is None:
        out_specs = [block]
        out_shape = [jax.ShapeDtypeStruct((4, size, columns), LOW)]
    else:
        in_specs.append(block)
        inputs.append(got)
        out_specs = [
            pl.BlockSpec((1, size, columns), lambda j, o: (jnp.minimum(j, 1), 0, 0)),
            pl.BlockSpec((1, size, columns), lambda j, o: (jnp.maximum(j, 2) - 2, 0, 0)),
        ]
        out_shape = [
            jax.ShapeDtypeStruct((2, size, columns), F32),
            jax.ShapeDtypeStruct((2, size, columns), LOW),
        ]
    kernel = functools.partial(row_grads_kernel, blocks, turned, got is not None)
    kernel = with_deps(kernel, len(inputs), len(deps), 1)
    in_specs += [pl.BlockSpec(memory_space=pl.ANY)] * len(deps)
    return pl.pallas_call(
        kernel,
        grid_spec=pltpu.PrefetchScalarGridSpec(
            num_scalar_prefetch=1, grid=(4,), in_specs=in_specs, out_specs=out_specs
        ),
        out_shape=out_shape,
        compiler_params=pltpu.CompilerParams(
            dimension_semantics=("arbitrary",), vmem_limit_bytes=VMEM_LIMIT
        ),
        cost_estimate=SMALL_COST,
        name=name,
    )(order, *inputs, *deps)


def project_back_kernel(blocks, groups, terms, peer_ref, *refs):
    q_refs, refs = refs[:groups], refs[groups:]
    term_refs, refs = refs[:terms], refs[terms:]
    cos_ref, sin_ref, w_ref = refs[:3]
    out_refs = refs[3 : 3 + blocks]
    d_projected_ref, turned, placed = refs[3 + blocks :]
    heads = q_refs[0].shape[0]
    rows = out_refs[0].shape[0]
    half = HD // 2

    @pl.when(pl.program_id(0) == 0)
    def _():
        for group in range(groups):
            d_projected_ref[group * heads : (group + 1) * heads] = q_refs[group][...]
            part = pl.ds(group * 2 * HD, 2 * HD)
            total = term_refs[0][part, :].astype(F32)
            for term_ref in term_refs[1:]:
                total = total + term_ref[part, :].astype(F32)
            first, second = total[:half], total[half:HD]
            key = groups * heads + group * HD
            d_projected_ref[key : key + half] = (
                first * cos_ref[...] + second * sin_ref[...]
            ).astype(LOW)
            d_projected_ref[key + half : key + HD] = (
                second * cos_ref[...] - first * sin_ref[...]
            ).astype(LOW)
            d_projected_ref[key + groups * HD : key + (groups + 1) * HD] = total[HD:].astype(LOW)
        turned[...] = d_projected_ref[...].T
        for block in range(blocks):
            start = pl.multiple_of(peer_ref[block] * rows, rows)
            placed[block * rows : (block + 1) * rows] = turned[pl.ds(start, rows)]

    store_blocks(out_refs, dot_nt(placed[...], w_ref[...]))


def project_back(peers, d_query, kv_terms, cosine, sine, weights, *deps):
    blocks, groups, terms = peers.shape[0], len(d_query), len(kv_terms)
    heads, tokens = d_query[0].shape
    columns = groups * (heads + 2 * HD)
    width = weights.shape[0]
    rows = tokens // blocks
    inputs = [*d_query, *kv_terms, cosine, sine]
    outs = pl.pallas_call(
        with_deps(
            functools.partial(project_back_kernel, blocks, groups, terms),
            len(inputs) + 1,
            len(deps),
            1,
        ),
        grid_spec=pltpu.PrefetchScalarGridSpec(
            num_scalar_prefetch=1,
            grid=(width // TILE,),
            in_specs=[pl.BlockSpec(each.shape, lambda j, o: (0, 0)) for each in inputs]
            + [pl.BlockSpec((TILE, columns), lambda j, o: (j, 0))]
            + [pl.BlockSpec(memory_space=pl.ANY)] * len(deps),
            out_specs=[pl.BlockSpec((rows, TILE), lambda j, o: (0, j))] * blocks
            + [pl.BlockSpec((columns, tokens), lambda j, o: (0, 0))],
            scratch_shapes=[
                pltpu.VMEM((tokens, columns), LOW),
                pltpu.VMEM((tokens, columns), LOW),
            ],
        ),
        out_shape=block_shapes(blocks, rows, width)
        + [jax.ShapeDtypeStruct((columns, tokens), LOW)],
        compiler_params=pltpu.CompilerParams(
            dimension_semantics=("arbitrary",), vmem_limit_bytes=VMEM_LIMIT
        ),
        cost_estimate=SMALL_COST,
        name="project_back",
    )(peers, *inputs, weights, *deps)
    return outs[:blocks], outs[blocks]


def place_rows_kernel(blocks, peer_ref, *refs):
    out_ref = refs[blocks]
    for block in range(blocks):

        @pl.when(pl.program_id(0) == block)
        def _(block=block):
            out_ref[...] = refs[block][...].astype(out_ref.dtype)


def place_rows(peers, blocks, dtype, *deps):
    count = len(blocks)
    rows, width = blocks[0].shape
    return pl.pallas_call(
        with_deps(functools.partial(place_rows_kernel, count), count, len(deps), 1),
        grid_spec=pltpu.PrefetchScalarGridSpec(
            num_scalar_prefetch=1,
            grid=(count,),
            in_specs=[pl.BlockSpec((rows, width), lambda j, o: (0, 0))] * count
            + [pl.BlockSpec(memory_space=pl.ANY)] * len(deps),
            out_specs=pl.BlockSpec((rows, width), lambda j, o: (o[j], 0)),
        ),
        out_shape=jax.ShapeDtypeStruct((count * rows, width), dtype),
        compiler_params=pltpu.CompilerParams(
            dimension_semantics=("arbitrary",), vmem_limit_bytes=VMEM_LIMIT
        ),
        cost_estimate=SMALL_COST,
        name="place_rows",
    )(peers, *blocks, *deps)


def project_out_kernel(blocks, parts, peer_ref, attn_ref, *refs):
    w_refs, out_refs = refs[:parts], refs[parts : parts + blocks]
    placed_ref, turned = refs[parts + blocks :]
    rows = out_refs[0].shape[0]

    @pl.when(pl.program_id(0) == 0)
    def _():
        turned[...] = attn_ref[...].T
        for block in range(blocks):
            start = pl.multiple_of(peer_ref[block] * rows, rows)
            placed_ref[block * rows : (block + 1) * rows] = turned[pl.ds(start, rows)]

    weights = jnp.concatenate([w_ref[...] for w_ref in w_refs], axis=1)
    store_blocks(out_refs, dot_nt(placed_ref[...], weights))


def project_out(peers, attn_in, weights, start):
    blocks = peers.shape[0]
    columns, tokens = attn_in.shape
    width = weights.shape[0]
    rows = tokens // blocks
    size = math.gcd(start, columns)
    parts = columns // size

    def part_spec(part):
        return pl.BlockSpec((TILE, size), lambda j, o: (j, start // size + part))

    outs = pl.pallas_call(
        functools.partial(project_out_kernel, blocks, parts),
        grid_spec=pltpu.PrefetchScalarGridSpec(
            num_scalar_prefetch=1,
            grid=(width // TILE,),
            in_specs=[pl.BlockSpec((columns, tokens), lambda j, o: (0, 0))]
            + [part_spec(part) for part in range(parts)],
            out_specs=[pl.BlockSpec((rows, TILE), lambda j, o: (0, j))] * blocks
            + [pl.BlockSpec((tokens, columns), lambda j, o: (0, 0))],
            scratch_shapes=[pltpu.VMEM((tokens, columns), LOW)],
        ),
        out_shape=block_shapes(blocks, rows, width)
        + [jax.ShapeDtypeStruct((tokens, columns), LOW)],
        compiler_params=pltpu.CompilerParams(
            dimension_semantics=("arbitrary",), vmem_limit_bytes=VMEM_LIMIT
        ),
        cost_estimate=pl.CostEstimate(
            flops=3 * tokens * columns * width,
            bytes_accessed=4 * width * columns,
            transcendentals=0,
        ),
        name="project_out",
    )(peers, attn_in, *([weights] * parts))
    return outs[:blocks], outs[blocks]


def mix_back_kernel(blocks, parts, peer_ref, *refs):
    mid_refs, w_refs = refs[:blocks], refs[blocks : blocks + parts]
    out_ref, summed, placed = refs[blocks + parts :]
    rows = mid_refs[0].shape[0]
    mid = jnp.concatenate([mid_ref[...] for mid_ref in mid_refs], axis=0)
    weights = jnp.concatenate([w_ref[...] for w_ref in w_refs], axis=1)
    product = dot_nn(mid, weights)

    @pl.when(pl.program_id(0) == 0)
    def _():
        summed[...] = product

    @pl.when(pl.program_id(0) > 0)
    def _():
        summed[...] += product

    @pl.when(pl.program_id(0) == pl.num_programs(0) - 1)
    def _():
        for block in range(blocks):
            start = pl.multiple_of(peer_ref[block] * rows, rows)
            placed[pl.ds(start, rows)] = summed[block * rows : (block + 1) * rows].astype(LOW)
        out_ref[...] = placed[...].T


def mix_back(peers, mid_blocks, weights, start, columns):
    blocks = len(mid_blocks)
    rows, width = mid_blocks[0].shape
    tokens = rows * blocks
    depth = 2 * TILE
    size = math.gcd(start, columns)
    parts = columns // size

    def part_spec(part):
        return pl.BlockSpec((depth, size), lambda j, o: (j, start // size + part))

    return pl.pallas_call(
        functools.partial(mix_back_kernel, blocks, parts),
        grid_spec=pltpu.PrefetchScalarGridSpec(
            num_scalar_prefetch=1,
            grid=(width // depth,),
            in_specs=[pl.BlockSpec((rows, depth), lambda j, o: (0, j))] * blocks
            + [part_spec(part) for part in range(parts)],
            out_specs=pl.BlockSpec((columns, tokens), lambda j, o: (0, 0)),
            scratch_shapes=[pltpu.VMEM((tokens, columns), F32), pltpu.VMEM((tokens, columns), LOW)],
        ),
        out_shape=jax.ShapeDtypeStruct((columns, tokens), LOW),
        compiler_params=pltpu.CompilerParams(
            dimension_semantics=("arbitrary",), vmem_limit_bytes=VMEM_LIMIT
        ),
        cost_estimate=pl.CostEstimate(
            flops=3 * tokens * columns * width,
            bytes_accessed=4 * width * columns,
            transcendentals=0,
        ),
        name="mix_back",
    )(peers, *mid_blocks, *([weights] * parts))


def is_square():
    return lax.axis_size("dp") == 2 and lax.axis_size("ctx") == 4


def swap_core(values):
    return lax.ppermute(values, "ctx", flip_pairs(4, 1))


def swap_across(values):
    return lax.ppermute(values, "ctx", flip_pairs(4, 2))


def swap_along(values):
    return lax.ppermute(values, "dp", flip_pairs(2, 1))


def owner_order(core_flip, across_first):
    along, ctx = lax.axis_index("dp"), lax.axis_index("ctx")
    order = []
    for block in range(4):
        high, low = block >> 1, block & 1
        flip_x, flip_y = (high, low) if across_first else (low, high)
        order.append(((along ^ flip_y) << 2) | (ctx ^ (flip_x << 1) ^ core_flip))
    return jnp.stack(order).astype(jnp.int32)


def travel_open(left_blocks, right, turned, across_first, name, *deps):
    far = row_grads(
        left_blocks, right, turned, owner_order(1, across_first), None, name + "_far", *deps
    )[0]
    return swap_core(far)


def travel_cross(left_blocks, right, turned, across_first, got, name, *deps):
    kept, sent = row_grads(
        left_blocks, right, turned, owner_order(0, across_first), got, name + "_near", *deps
    )
    swap = swap_across if across_first else swap_along
    return kept, swap(sent)


def travel_last(kept, got, across_first):
    swap = swap_along if across_first else swap_across
    total = kept + got.astype(F32)
    return [total[0], swap(total[1].astype(LOW))]


def small_grads_kernel(one_ref, mid_ref, d_projected_ref, attn_ref, grads_ref):
    split = d_projected_ref.shape[0]
    grads_ref[:, :split] = dot_nt(one_ref[...].T, d_projected_ref[...]).astype(LOW)
    grads_ref[:, split:] = dot_nn(mid_ref[...].T, attn_ref[...]).astype(LOW)


def small_grads(normed_one, d_mid_low, d_projected, attn_in):
    tokens, width = normed_one.shape
    columns = d_projected.shape[0] + attn_in.shape[1]
    return tile_call(
        small_grads_kernel,
        "small_grads",
        width // TILE,
        [pl.BlockSpec((tokens, TILE), lambda j: (0, j))] * 2
        + [whole(d_projected.shape), whole(attn_in.shape)],
        [pl.BlockSpec((TILE, columns), lambda j: (j, 0))],
        [jax.ShapeDtypeStruct((width, columns), LOW)],
        2 * tokens * width * columns,
    )(normed_one, d_mid_low, d_projected, attn_in)[0]


def adamw_kernel(turned, step_rate, w_ref, first_ref, second_ref, *refs):
    grad_refs, out_refs, mark_ref = refs[:-4], refs[-4:-1], refs[-1]
    mark_ref[...] = jnp.zeros_like(mark_ref)
    gradient = grad_refs[0][...].astype(F32)
    for grad_ref in grad_refs[1:]:
        gradient = gradient + grad_ref[...].astype(F32)
    if turned:
        gradient = gradient.T
    results = adamw_step(
        w_ref[...], first_ref[...], second_ref[...], gradient, step_rate, WEIGHT_DECAY
    )
    for out_ref, result in zip(out_refs, results):
        out_ref[...] = result


def adamw_call(weight, first, second, terms, start, turned, step_rate, name, *deps):
    rows, columns = weight.shape
    long = rows if turned else columns
    size = math.gcd(math.gcd(start, long), 1024)
    if turned:
        spec = pl.BlockSpec((size, columns), lambda j: (j, 0))
    else:
        spec = pl.BlockSpec((rows, size), lambda j: (0, j))
    grad_specs = [
        pl.BlockSpec((term.shape[0], size), lambda j: (0, j + start // size)) for term in terms
    ]
    return tile_call(
        functools.partial(adamw_kernel, turned, step_rate),
        name,
        long // size,
        [spec, spec, spec] + grad_specs,
        [spec] * 3 + [whole((8, 128))],
        [jax.ShapeDtypeStruct(weight.shape, F32)] * 3 + [jax.ShapeDtypeStruct((8, 128), F32)],
        20 * weight.size,
        deps=len(deps),
    )(weight, first, second, *terms, *deps)


def local(
    hidden_in,
    positions,
    cotangent,
    w_qkv,
    w_qkv_first,
    w_qkv_second,
    w_out,
    w_out_first,
    w_out_second,
    w_gate_up,
    w_gate_up_first,
    w_gate_up_second,
    w_down,
    w_down_first,
    w_down_second,
    norm_gains,
    norm_gains_first,
    norm_gains_second,
):
    tensor_count = lax.axis_size("tensor")
    tensor_here = lax.axis_index("tensor")
    ctx_here = lax.axis_index("ctx")
    heads_here = HQ // tensor_count
    kv_here = KV // tensor_count
    head_ratio = HQ // KV
    units_here = FF // tensor_count
    q_cols = heads_here * HD
    k_cols = kv_here * HD
    tok_rows = hidden_in.shape[1]
    seq_rows = positions.shape[1]
    own_rows = tok_rows // tensor_count
    place_row = positions[0]
    query_places = lax.dynamic_slice_in_dim(place_row, ctx_here * tok_rows, tok_rows)
    run_ranks = place_row[::RUN] // RUN
    runs = seq_rows // RUN
    order = jnp.sum(
        jnp.where(
            run_ranks[None, :] == jnp.arange(runs, dtype=jnp.int32)[:, None],
            jnp.arange(runs, dtype=jnp.int32)[None, :],
            0,
        ),
        axis=1,
    ).astype(jnp.int32)
    query_ranks = query_places[::RUN] // RUN

    small_shard = jnp.concatenate([w_qkv.astype(LOW), w_out.astype(LOW).T], axis=1)
    full_small = lax.all_gather(small_shard, ("dp", "ctx"), axis=0, tiled=True)
    full_qkv = full_small[:, : q_cols + 2 * k_cols]
    ffn_shard = jnp.concatenate([w_gate_up.astype(LOW), w_down.astype(LOW).T], axis=1)
    full_ffn = lax.all_gather(ffn_shard, ("dp", "ctx"), axis=0, tiled=True)
    stacked = spread(spread(norm_gains.astype(LOW).astype(F32)[None], "ctx"), "dp")
    gain_values = jnp.swapaxes(stacked, 0, 1).reshape(norm_gains.shape[0], -1)

    hidden = hidden_in[0]
    grad_top = cotangent[0]
    own_start = tensor_here * own_rows
    hidden_own = lax.dynamic_slice_in_dim(hidden, own_start, own_rows).astype(F32)
    grad_own = lax.dynamic_slice_in_dim(grad_top, own_start, own_rows).astype(F32)

    x_hat_one, factor_one = normalize(hidden.astype(F32))
    normed_one = (x_hat_one * gain_values[0]).astype(LOW)
    projected = contract(full_qkv, normed_one, 0, 1)
    cosine, sine = rotary_tables(query_places)
    queries = (
        rotate(projected[:q_cols].reshape(kv_here, head_ratio, HD, tok_rows), cosine, sine)
        * SCORE_SCALE
    ).astype(LOW)
    keys_here = rotate(
        projected[q_cols : q_cols + k_cols].reshape(kv_here, HD, tok_rows), cosine, sine
    ).astype(LOW)
    values_here = projected[q_cols + k_cols :].reshape(kv_here, HD, tok_rows).astype(LOW)
    kv_local = jnp.concatenate([keys_here, values_here], axis=1)
    ctx_peers, tensor_peers = axis_peers("ctx"), axis_peers("tensor")
    kv_blocks = gather_blocks(kv_local, "ctx")
    mixed, attn_low, log_total = attend_forward(order, query_ranks, ctx_peers, queries, kv_blocks)

    def from_here(values, axis=0):
        return blocks_from_here(tensor_count, tensor_here, own_rows, values, axis)

    grad_top = from_here(grad_top)
    out_start = q_cols + 2 * k_cols
    out_parts, attn_in = project_out(
        tensor_peers, attn_low.reshape(q_cols, tok_rows), full_small, out_start
    )
    middle = hidden_own + sum_scatter(out_parts, "tensor")
    x_hat_two, factor_two = normalize(middle)
    normed_two = gather_blocks((x_hat_two * gain_values[1]).astype(LOW), "tensor")
    active, d_gate, d_up, d_two_parts = ffn_both(normed_two, grad_top, full_ffn)
    d_two_pieces = scatter_begin(d_two_parts, "tensor")
    ffn_parts = list(ffn_out(tensor_count, active, full_ffn, d_two_parts[0]))
    d_two_pieces[2], ffn_parts[0] = lax.optimization_barrier((d_two_pieces[2], ffn_parts[0]))
    d_two_pieces = scatter_middle(d_two_pieces, "tensor")
    grad_ffn, mark = ffn_grads(normed_two, grad_top, active, d_gate, d_up, ffn_parts[0])
    d_two_pieces[1:], mark = lax.optimization_barrier((d_two_pieces[1:], mark))
    grad_ffn = held_until(grad_ffn, d_two_pieces[-1])
    red_ffn = lax.optimization_barrier(
        lax.psum_scatter(grad_ffn, ("dp", "ctx"), scatter_dimension=0, tiled=True)
    )
    d_normed_two = scatter_end(d_two_pieces)

    grad_gain_two = jnp.sum(d_normed_two * x_hat_two, axis=0)
    d_middle = grad_own + norm_back(d_normed_two * gain_values[1], x_hat_two, factor_two)
    d_mid_blocks = gather_blocks(d_middle.astype(LOW), "tensor")
    d_mixed = mix_back(tensor_peers, d_mid_blocks, full_small, out_start, q_cols).reshape(
        kv_here, head_ratio, HD, tok_rows
    )
    mark, ffn_parts = lax.optimization_barrier((d_mid_blocks[3:], ffn_parts))
    ffn_pieces = scatter_begin(ffn_parts, "tensor")
    d_query, kv_terms = [], []
    for group in range(kv_here):
        d_heads, *kv_terms = attend_backward(
            group, order, query_ranks, ctx_peers, kv_blocks, kv_terms, queries, d_mixed, mixed,
            log_total, cosine, sine, *mark,
        )
        if group == 0:
            kv_terms, ffn_pieces[1:3] = lax.optimization_barrier((kv_terms, ffn_pieces[1:3]))
            ffn_pieces = scatter_middle(ffn_pieces, "tensor")
        d_query.append(d_heads.reshape(-1, tok_rows))
    kv_terms, ffn_pieces = lax.optimization_barrier((kv_terms, ffn_pieces))
    kv_pieces = scatter_begin(kv_terms, "ctx")
    if is_square():
        out_got = travel_open(d_mid_blocks, attn_in, False, True, "grads_out", kv_terms[0])
    block_own = (middle + scatter_end(ffn_pieces)).astype(LOW)
    if tensor_count == 4:
        block_far = lax.ppermute(block_own, "tensor", flip_pairs(4, 2))
        block_near = lax.ppermute(block_own, "tensor", flip_pairs(4, 1))
    else:
        block_blocks = gather_blocks(block_own, "tensor")

    kv_pieces = scatter_middle(kv_pieces, "ctx")
    if tensor_count == 4:
        kv_pieces[-1], block_far, block_near = lax.optimization_barrier(
            (kv_pieces[-1], block_far, block_near)
        )
    d_one_parts, d_projected = project_back(
        tensor_peers, d_query, kv_pieces, cosine, sine, full_small
    )
    d_one_pieces = scatter_begin(d_one_parts, "tensor")
    adamw_down = functools.partial(
        adamw_call, w_down, w_down_first, w_down_second, [red_ffn], 2 * units_here, True,
        LEARN_RATE, "adamw_down",
    )
    adamw_gate_up = functools.partial(
        adamw_call, w_gate_up, w_gate_up_first, w_gate_up_second, [red_ffn], 0, False,
        LEARN_RATE, "adamw_gate_up",
    )
    if is_square():
        out_kept, out_got = travel_cross(
            d_mid_blocks, attn_in, False, True, out_got, "grads_out", d_one_parts[0]
        )
        d_one_pieces[2], out_kept = lax.optimization_barrier((d_one_pieces[2], out_kept))
        d_one_pieces = scatter_middle(d_one_pieces, "tensor")
        qkv_far = row_grads(
            [normed_one], d_projected, True, owner_order(1, False), None, "grads_qkv_far", out_kept
        )[0]
        d_one_pieces[1:], out_kept, qkv_far = lax.optimization_barrier(
            (d_one_pieces[1:], out_kept, qkv_far)
        )
        qkv_got = swap_core(qkv_far)
    else:
        grad_small = small_grads(
            normed_one, jnp.concatenate(d_mid_blocks, axis=0), d_projected, attn_in
        )
        d_one_pieces = scatter_middle(d_one_pieces, "tensor")
        red_small = lax.optimization_barrier(
            lax.psum_scatter(grad_small, ("dp", "ctx"), scatter_dimension=0, tiled=True)
        )
    d_normed_one = scatter_end(d_one_pieces)
    x_hat_own, factor_own = normalize(hidden_own)
    grad_gain_one = jnp.sum(d_normed_one * x_hat_own, axis=0)
    grad_in_own = d_middle + norm_back(d_normed_one * gain_values[0], x_hat_own, factor_own)
    grad_in_low = grad_in_own.astype(LOW)
    gain_rows = jnp.stack([grad_gain_one, grad_gain_two])
    if is_square():
        qkv_kept, qkv_got = travel_cross(
            [normed_one], d_projected, True, False, qkv_got, "grads_qkv"
        )
    gu_first, gu_second, gu_new, mark = adamw_gate_up(d_normed_one)
    if tensor_count == 4:
        near = lax.ppermute(grad_in_low, "tensor", flip_pairs(4, 1))
        far = lax.ppermute(grad_in_low, "tensor", flip_pairs(4, 2))
        near, far, mark, gain_rows, block_far = lax.optimization_barrier(
            (near, far, mark, gain_rows, block_far)
        )
        if is_square():
            near, out_got, qkv_kept = lax.optimization_barrier((near, out_got, qkv_kept))
        grad_in_blocks = [grad_in_low, near, far, lax.ppermute(far, "tensor", flip_pairs(4, 1))]
        block_last = lax.ppermute(block_far, "tensor", flip_pairs(4, 1))
        block_blocks = [block_own, block_near, block_far, block_last]
    else:
        grad_in_blocks = gather_blocks(grad_in_low, "tensor")
    small_start = 0
    if not is_square():
        small_start, out_terms, qkv_terms = out_start, [red_small], [red_small]
    else:
        out_terms = travel_last(out_kept, out_got, True)
        qkv_terms = travel_last(qkv_kept, qkv_got, False)
    down_first, down_second, down_new, mark = adamw_down(mark)
    out_first, out_second, out_new, mark = adamw_call(
        w_out, w_out_first, w_out_second, out_terms, small_start, True, OUT_RATE, "adamw_out", mark
    )
    gain_sums = sum_everywhere(gain_rows, "tensor")
    gain_parts = jnp.swapaxes(gain_sums.reshape(2, -1, norm_gains.shape[1]), 0, 1)
    red_gains = gains_scatter(gains_scatter(gain_parts, "dp"), "ctx")[0]
    grad_in_blocks[3], red_gains = lax.optimization_barrier((grad_in_blocks[3], red_gains))
    qkv_first, qkv_second, qkv_new, last_mark = adamw_call(
        w_qkv, w_qkv_first, w_qkv_second, qkv_terms, 0, False, LEARN_RATE, "adamw_qkv", mark
    )
    grad_in = place_rows(tensor_peers, grad_in_blocks, F32, block_blocks[3], mark)
    grad_in = grad_in.reshape(hidden_in.shape)
    block_out = place_rows(tensor_peers, block_blocks, LOW).reshape(hidden_in.shape)
    gain_first, gain_second, gain_new = adamw_step(
        norm_gains, norm_gains_first, norm_gains_second, red_gains, GAIN_RATE, 0.0
    )
    return (
        block_out,
        grad_in,
        qkv_first,
        qkv_second,
        qkv_new,
        out_first,
        out_second,
        out_new,
        gu_first,
        gu_second,
        gu_new,
        down_first,
        down_second,
        down_new,
        gain_first,
        gain_second,
        gain_new,
    )


def solution(mesh):
    tokens = P("dp", "ctx", None)
    rows = P(("dp", "ctx"), "tensor")
    columns = P("tensor", ("dp", "ctx"))
    gains = P(None, ("dp", "ctx"))
    placed = (
        (tokens, P("dp", None), tokens)
        + (rows,) * 3
        + (columns,) * 3
        + (rows,) * 3
        + (columns,) * 3
        + (gains,) * 3
    )
    return jax.shard_map(
        local,
        mesh=mesh,
        in_specs=placed,
        out_specs=(tokens, tokens) + placed[3:],
        check_vma=False,
    )
```
